32 devices in a mesh: seq: 8 (over z, y), head: 4 (over x, core).
Axes of the slice: x: 2, y: 2, z: 4, core: 2. Of those that a mesh axis runs over, the one named last changes fastest.
Arguments:
- queries: bfloat16 [2048, 2048], P(('seq', 'head')), may hold values from -25 to 25
- keys: bfloat16 [2048, 2048], P(('seq', 'head')), may hold values from -6 to 6
- values: bfloat16 [2048, 2048], P(('seq', 'head')), may hold values from -12 to 12
- cotangent: bfloat16 [2048, 2048], P(('seq', 'head')), may hold values from -6 to 6
- random_blocks: int32 [32, 3], P('seq'), may hold values from 0 to 31, as said below
- global_blocks: int32 [2], replicated, may hold values from 0 to 31
Outputs:
- attention_out: bfloat16 [2048, 2048], P('seq', 'head')
- grad_queries: bfloat16 [2048, 2048], P('seq', 'head')
- grad_keys: bfloat16 [2048, 2048], P('seq', 'head')
- grad_values: bfloat16 [2048, 2048], P('seq', 'head')
The draws below stay inside these ranges and needn't reach their ends.
Inputs may be any that keep to these rules, and one draw needn't show every extreme that they name: `random_blocks`: block numbers of the document. Block c is held by seq index c // 4. Among the 12 entries of the query blocks of one seq index (aligned groups of 4 rows), at most 3 name blocks held by any one seq index; in every draw some seq index has its blocks named exactly 3 times by the entries of every seq index.
All inputs are finite; a program needn't handle non-finite values.
Results may differ from the reference program's by a relative error of at most 0.0052.
Values may be sent and summed in bfloat16 or wider, within the bound.
A program may use at most 128 MiB of HBM per device.

```python
import math
import jax
import jax.numpy as jnp
from jax import lax

HEAD_SIZE = 128
BLOCK_TOKENS = 64
GLOB = 2
RAND = 3
BLK_DEV = 4
SHARDS = 8
NB = 32
TOKENS = 2048
FEAT = 2048
REQ = 12
CAP = 3
LOW = 2


def draw_queries(key, part):
    drawn = 2.5 * jax.random.truncated_normal(jax.random.fold_in(key, 3), -6.0, 6.0, (TOKENS, FEAT), jnp.float32)
    return drawn.astype(jnp.bfloat16)


def draw_keys(key, part):
    drawn = jax.random.truncated_normal(jax.random.fold_in(key, 5), -6.0, 6.0, (TOKENS, FEAT), jnp.float32)
    return drawn.astype(jnp.bfloat16)


def draw_random_blocks(key, part):
    hot_owner = jax.random.randint(jax.random.fold_in(key, 35), (), 0, SHARDS)
    counts = jax.random.randint(jax.random.fold_in(key, 31), (SHARDS, SHARDS), LOW, CAP + 1)
    counts = counts.at[:, 0].set(CAP)
    ends = jnp.cumsum(counts, axis=1)
    entry = jnp.arange(REQ)
    bins = jnp.sum((ends[:, None, :] <= entry[None, :, None]).astype(jnp.int32), axis=2)
    others = jax.vmap(lambda sub: jax.random.permutation(sub, SHARDS - 1))(jax.random.split(jax.random.fold_in(key, 32), SHARDS))
    picked = jnp.take_along_axis(others, jnp.clip(bins - 1, 0, SHARDS - 2), axis=1)
    owners = jnp.where(bins == 0, hot_owner, (hot_owner + 1 + picked) % SHARDS)
    local_ids = jax.random.randint(jax.random.fold_in(key, 33), (SHARDS, REQ), 0, BLK_DEV)
    block_ids = owners * BLK_DEV + local_ids
    order = jax.vmap(lambda sub: jax.random.permutation(sub, REQ))(jax.random.split(jax.random.fold_in(key, 34), SHARDS))
    shuffled = jnp.take_along_axis(block_ids, order, axis=1)
    return shuffled.reshape(NB, RAND).astype(jnp.int32)


def block_levels(stream_key, shape, cuts, least, top_value):
    loudness, own = 1.0, jax.random.fold_in(stream_key, 6)
    for dim, parts in cuts:
        steps = jnp.exp(jax.random.uniform(jax.random.fold_in(own, dim), (parts,), jnp.float32, least / len(cuts), top_value / len(cuts)))
        loudness = loudness * jnp.repeat(steps, shape[dim] // parts).reshape([-1 if axis == dim else 1 for axis in range(len(shape))])
    return loudness


def scatter_about(own_key, extent, scale, bound, cuts=(), kind=jnp.bfloat16):
    values = jax.random.normal(own_key, extent, jnp.float32) * scale
    if len(cuts) > 0:
        values = block_levels(own_key, extent, cuts, -0.22, 0.18) * values
    return jnp.clip(values, min=-bound, max=bound).astype(kind)


def setup_inputs(seed: int = 0) -> dict:
    streams_of = jax.random.split(jax.random.key(seed), 7)
    queries = draw_queries(jax.random.fold_in(streams_of[6], 71), 0)
    keys = draw_keys(jax.random.fold_in(streams_of[6], 71), 0)
    values = scatter_about(streams_of[2], (TOKENS, FEAT), 2.0, 12.0, ((0, 32),))
    cotangent = scatter_about(streams_of[3], (TOKENS, FEAT), 1.0, 6.0, ((0, 32),))
    random_blocks = draw_random_blocks(jax.random.fold_in(streams_of[6], 71), 0)
    global_blocks = jax.random.randint(streams_of[5], (GLOB,), 0, NB).astype(jnp.int32)
    return {"queries": queries, "keys": keys, "values": values, "cotangent": cotangent, "random_blocks": random_blocks, "global_blocks": global_blocks}


NEG_FILL = -1e+30

def reference(queries, keys, values, cotangent, random_blocks, global_blocks):
    block_total = TOKENS // BLOCK_TOKENS
    head_count = FEAT // HEAD_SIZE
    key_block_sets = 3 + GLOB + RAND
    logit_scale = 1.0 / math.sqrt(HEAD_SIZE)
    block_ids = jnp.arange(block_total, dtype=jnp.int32)
    band_table = jnp.stack([block_ids - 1, block_ids, block_ids + 1], axis=1)
    band_valid = (band_table >= 0) & (band_table < block_total)
    band_table = jnp.clip(band_table, 0, block_total - 1).astype(jnp.int32)
    global_table = jnp.broadcast_to(global_blocks.astype(jnp.int32)[None, :], (block_total, GLOB))
    key_table = jnp.concatenate([band_table, global_table, random_blocks.astype(jnp.int32)], axis=1)
    valid_keys = jnp.concatenate([band_valid, jnp.ones((block_total, GLOB + RAND), dtype=bool)], axis=1)
    valid_keys = jnp.repeat(valid_keys, BLOCK_TOKENS, axis=1)[:, None, :]

    def by_head(array):
        return array.reshape(block_total, BLOCK_TOKENS, head_count, HEAD_SIZE).transpose(2, 0, 1, 3)

    def round_random(terms):
        fixed = terms[:, :3 + GLOB]
        rounded = lax.optimization_barrier(terms[:, 3 + GLOB:].astype(jnp.bfloat16)).astype(jnp.float32)
        return jnp.concatenate([fixed, rounded], axis=1)

    def one_head(items):
        query_head, key_head, value_head, cotan_head = items
        gathered_keys = key_head[key_table].reshape(block_total, key_block_sets * BLOCK_TOKENS, HEAD_SIZE).astype(jnp.float32)
        gathered_values = value_head[key_table].reshape(block_total, key_block_sets * BLOCK_TOKENS, HEAD_SIZE).astype(jnp.float32)
        query_wide = query_head.astype(jnp.float32)
        cotangent_wide = cotan_head.astype(jnp.float32)
        score_matrix = jnp.einsum('nwx,ntx->nwt', query_wide, gathered_keys) * logit_scale
        score_matrix = jnp.where(valid_keys, score_matrix, NEG_FILL)
        row_peak = lax.optimization_barrier(jnp.max(score_matrix, axis=-1, keepdims=True))
        exponent = jnp.exp(score_matrix - row_peak)
        weights = exponent / lax.optimization_barrier(jnp.sum(exponent, axis=-1, keepdims=True))
        weights_low = weights.astype(jnp.bfloat16)
        recomputed_weights = weights_low.astype(jnp.float32)
        attended_output = jnp.einsum('lfo,loa->lfa', recomputed_weights, gathered_values).astype(jnp.bfloat16)
        weight_gradient = jnp.einsum('nwx,ntx->nwt', cotangent_wide, gathered_values)
        row_delta = lax.optimization_barrier(jnp.sum(weights * weight_gradient, axis=-1, keepdims=True))
        score_grad = (weights * (weight_gradient - row_delta) * logit_scale).astype(jnp.bfloat16)
        score_gradient = score_grad.astype(jnp.float32)
        query_gradient = jnp.einsum('lfo,loa->lfa', score_gradient, gathered_keys).astype(jnp.bfloat16)
        key_gradient_parts = jnp.einsum('mtn,mti->mni', score_gradient, query_wide).reshape(block_total, key_block_sets, BLOCK_TOKENS, HEAD_SIZE)
        value_gradient_parts = jnp.einsum('mtn,mti->mni', recomputed_weights, cotangent_wide).reshape(block_total, key_block_sets, BLOCK_TOKENS, HEAD_SIZE)
        key_gradient_parts = round_random(key_gradient_parts)
        value_gradient_parts = round_random(value_gradient_parts)
        grad_key = jnp.zeros((block_total, BLOCK_TOKENS, HEAD_SIZE), jnp.float32).at[key_table].add(key_gradient_parts).astype(jnp.bfloat16)
        grad_value = jnp.zeros((block_total, BLOCK_TOKENS, HEAD_SIZE), jnp.float32).at[key_table].add(value_gradient_parts).astype(jnp.bfloat16)
        return (attended_output, query_gradient, grad_key, grad_value)
    results = lax.map(one_head, (by_head(queries), by_head(keys), by_head(values), by_head(cotangent)))

    def merge_heads(array):
        return array.transpose(1, 2, 0, 3).reshape(TOKENS, FEAT)
    return (merge_heads(results[0]), merge_heads(results[1]), merge_heads(results[2]), merge_heads(results[3]))
```

```python
import functools
import math

import jax
import jax.numpy as jnp
from jax import lax
from jax.experimental import pallas as pl
from jax.experimental.pallas import tpu as pltpu
from jax.sharding import PartitionSpec as P

HEAD_SIZE = 128
BLOCK_TOKENS = 64
GLOB = 2
RAND = 3


NEG_FILL = -1e30


def padded(shard, sides, width):
    for axis, dim in sides:
        size, length = (lax.axis_size(axis), shard.shape[dim])
        up = [(i, (i + 1) % size) for i in range(size - 1)]
        down = [(j, i) for i, j in up]
        last = lax.slice_in_dim(shard, length - width, length, axis=dim)
        leading = lax.slice_in_dim(shard, 0, width, axis=dim)
        before = lax.ppermute(last, axis, up)
        after = lax.ppermute(leading, axis, down)
        shard = jnp.concatenate([before, shard, after], axis=dim)
    return shard


def broadcast(block, axis, source):
    block = jnp.where(lax.axis_index(axis) == source, block, jnp.zeros_like(block))
    return lax.psum(block, axis)


def entry_ranks(owner_ids):
    count = owner_ids.shape[-1]
    earlier = jnp.arange(count)[None, :] < jnp.arange(count)[:, None]
    same_owner = owner_ids[..., :, None] == owner_ids[..., None, :]
    return jnp.sum((same_owner & earlier).astype(jnp.int32), axis=-1)


def spread_band(band_part):
    return (
        jnp.pad(band_part[:, 0], ((0, 2), (0, 0), (0, 0)))
        + jnp.pad(band_part[:, 1], ((1, 1), (0, 0), (0, 0)))
        + jnp.pad(band_part[:, 2], ((2, 0), (0, 0), (0, 0)))
    )


def shards(queries, keys, values, cotangent, random_blocks, global_blocks):
    query_rows, gathered_keys, gathered_values, cotan_rows = (
        lax.all_to_all(queries, "head", split_axis=1, concat_axis=0, tiled=True),
        lax.all_to_all(keys, "head", split_axis=1, concat_axis=0, tiled=True),
        lax.all_to_all(values, "head", split_axis=1, concat_axis=0, tiled=True),
        lax.all_to_all(cotangent, "head", split_axis=1, concat_axis=0, tiled=True),
    )
    row_count, width = query_rows.shape
    head_count = width // HEAD_SIZE
    block_count = row_count // BLOCK_TOKENS
    shard_count = lax.axis_size("seq")
    my_index = lax.axis_index("seq")
    entry_count = block_count * RAND
    slot_cap = (3 * entry_count + 2 * shard_count - 1) // (2 * shard_count)
    slot_count = shard_count * slot_cap
    key_block_sets = 3 + GLOB + RAND
    logit_scale = 1.0 / math.sqrt(HEAD_SIZE)
    key_value = jnp.stack([gathered_keys, gathered_values])
    widened = padded(key_value, (("seq", 1),), BLOCK_TOKENS)
    widened = widened.reshape(2, block_count + 2, BLOCK_TOKENS, width)
    band_rows = jnp.stack([widened[:, :-2], widened[:, 1:-1], widened[:, 2:]], axis=2)
    own_blocks = key_value.reshape(2, block_count, BLOCK_TOKENS, width)
    owner_global = global_blocks // block_count
    local_global = global_blocks % block_count
    fetched = []
    for number in range(GLOB):
        mine = jnp.take(own_blocks, local_global[number], axis=1)
        fetched.append(broadcast(mine, "seq", owner_global[number]))
    global_rows = jnp.stack(fetched, axis=1)
    entry_ids = random_blocks.reshape(entry_count)
    owner_ids = entry_ids // block_count
    slot_ids = owner_ids * slot_cap + entry_ranks(owner_ids)
    slot_hits = slot_ids[None, :] == jnp.arange(slot_count)[:, None]
    filled = jnp.any(slot_hits, axis=1)
    source = jnp.sum(jnp.where(slot_hits, jnp.arange(entry_count)[None, :], 0), axis=1)
    wanted = jnp.sum(jnp.where(slot_hits, (entry_ids % block_count)[None, :], 0), axis=1)
    asked_ids = lax.all_to_all(wanted, "seq", split_axis=0, concat_axis=0, tiled=True)
    outgoing = jnp.take(own_blocks, asked_ids, axis=1)
    incoming = lax.all_to_all(outgoing, "seq", split_axis=1, concat_axis=1, tiled=True)
    random_rows = jnp.take(incoming, slot_ids, axis=1).reshape(
        2, block_count, RAND, BLOCK_TOKENS, width
    )

    def assemble_keys(which):
        spread_global = jnp.broadcast_to(
            global_rows[which][None], (block_count, GLOB, BLOCK_TOKENS, width)
        )
        joined = jnp.concatenate([band_rows[which], spread_global, random_rows[which]], axis=1)
        return joined.reshape(block_count, key_block_sets * BLOCK_TOKENS, head_count, HEAD_SIZE)

    key_all = assemble_keys(0)
    value_all = assemble_keys(1)
    block_number = my_index * block_count + jnp.arange(block_count)
    total_blocks = shard_count * block_count
    always = jnp.ones((block_count,), dtype=bool)
    group_ok = jnp.stack(
        [block_number >= 1, always, block_number <= total_blocks - 2] + [always] * (GLOB + RAND),
        axis=1,
    )
    valid_keys = jnp.repeat(group_ok, BLOCK_TOKENS, axis=1)[:, None, None, :]
    query_blocks = query_rows.reshape(block_count, BLOCK_TOKENS, head_count, HEAD_SIZE)
    cotan_blocks = cotan_rows.reshape(block_count, BLOCK_TOKENS, head_count, HEAD_SIZE)
    score_matrix = (
        jnp.einsum("bqhd,bkhd->bhqk", query_blocks, key_all, preferred_element_type=jnp.float32)
        * logit_scale
    )
    score_matrix = jnp.where(valid_keys, score_matrix, NEG_FILL)
    row_peak = jnp.max(score_matrix, axis=-1, keepdims=True)
    exponent = jnp.exp(score_matrix - row_peak)
    weights = exponent / jnp.sum(exponent, axis=-1, keepdims=True)
    weights_low = weights.astype(jnp.bfloat16)
    attended_output = jnp.einsum(
        "bhqk,bkhd->bqhd", weights_low, value_all, preferred_element_type=jnp.float32
    ).astype(jnp.bfloat16)
    weight_gradient = jnp.einsum(
        "bqhd,bkhd->bhqk", cotan_blocks, value_all, preferred_element_type=jnp.float32
    )
    row_delta = jnp.sum(weights * weight_gradient, axis=-1, keepdims=True)
    score_grad = (weights * (weight_gradient - row_delta) * logit_scale).astype(jnp.bfloat16)
    query_gradient = jnp.einsum(
        "bhqk,bkhd->bqhd", score_grad, key_all, preferred_element_type=jnp.float32
    ).astype(jnp.bfloat16)

    def part_grads(first, count):
        low_key = first * BLOCK_TOKENS
        high_key = (first + count) * BLOCK_TOKENS
        key_part = jnp.einsum(
            "bhqk,bqhd->bkhd",
            score_grad[..., low_key:high_key],
            query_blocks,
            preferred_element_type=jnp.float32,
        )
        value_part = jnp.einsum(
            "bhqk,bqhd->bkhd",
            weights_low[..., low_key:high_key],
            cotan_blocks,
            preferred_element_type=jnp.float32,
        )
        return (
            key_part.reshape(block_count, count, BLOCK_TOKENS, width),
            value_part.reshape(block_count, count, BLOCK_TOKENS, width),
        )

    band_key, band_value = part_grads(0, 3)
    extended_key = spread_band(band_key)
    extended_value = spread_band(band_value)
    rim_pair = jnp.stack(
        [
            jnp.stack([extended_key[0], extended_key[-1]]),
            jnp.stack([extended_value[0], extended_value[-1]]),
        ]
    )
    rimmed = padded(rim_pair.astype(jnp.bfloat16), (("seq", 1),), 1).astype(rim_pair.dtype)
    key_local = extended_key[1:-1].at[0].add(rimmed[0, 0]).at[-1].add(rimmed[0, 3])
    value_local = extended_value[1:-1].at[0].add(rimmed[1, 0]).at[-1].add(rimmed[1, 3])
    global_key, global_value = part_grads(3, GLOB)
    total_key, total_value = lax.psum(
        (jnp.sum(global_key, axis=0), jnp.sum(global_value, axis=0)), "seq"
    )
    for number in range(GLOB):
        owned = owner_global[number] == my_index
        key_local = key_local.at[local_global[number]].add(jnp.where(owned, total_key[number], 0.0))
        value_local = value_local.at[local_global[number]].add(
            jnp.where(owned, total_value[number], 0.0)
        )
    random_key, random_value = part_grads(3 + GLOB, RAND)
    keep = filled[:, None, None]
    send_key = jnp.where(
        keep, jnp.take(random_key.reshape(entry_count, BLOCK_TOKENS, width), source, axis=0), 0.0
    ).astype(jnp.bfloat16)
    send_value = jnp.where(
        keep, jnp.take(random_value.reshape(entry_count, BLOCK_TOKENS, width), source, axis=0), 0.0
    ).astype(jnp.bfloat16)
    arrived_key, arrived_value = (
        lax.all_to_all(send_key, "seq", split_axis=0, concat_axis=0, tiled=True),
        lax.all_to_all(send_value, "seq", split_axis=0, concat_axis=0, tiled=True),
    )
    owner_hits = (asked_ids[None, :] == jnp.arange(block_count)[:, None]).astype(jnp.float32)
    key_local = key_local + jnp.einsum(
        "js,srf->jrf", owner_hits, arrived_key.astype(jnp.float32), precision=lax.Precision.HIGHEST
    )
    value_local = value_local + jnp.einsum(
        "js,srf->jrf",
        owner_hits,
        arrived_value.astype(jnp.float32),
        precision=lax.Precision.HIGHEST,
    )
    return (
        attended_output.reshape(row_count, width),
        query_gradient.reshape(row_count, width),
        key_local.reshape(row_count, width).astype(jnp.bfloat16),
        value_local.reshape(row_count, width).astype(jnp.bfloat16),
    )


MESH = pl.DeviceIdType.MESH
GROUP = 4


def contract(a, b, dim_a, dim_b):
    return lax.dot_general(
        a, b, (((dim_a,), (dim_b,)), ((), ())), preferred_element_type=jnp.float32
    )


def head_kernel(
    seq, heads, per_out,
    k_ref, q_ref, v_ref, g_ref, random_ref, global_ref,
    out_ref, dq_ref, dk_ref, dv_ref,
    kb, qb, vb, gb, cb, bias, dka, dva, dkr, dvr, stage,
    send_sem, recv_sem, own_sem, swap_send, swap_recv, grad_send, grad_recv,
    out_send, out_recv,
):
    s = lax.axis_index("seq")
    h = lax.axis_index("head")
    x, c = h // 2, h % 2
    planes = heads // 2
    chips = seq * planes
    devices = seq * heads
    me = s * heads + h
    place = s * planes + x
    sources = (k_ref, q_ref, v_ref, g_ref)
    landing = (kb.at[c], qb, vb.at[c], gb)
    sibling = (s, 2 * x + 1 - c)

    barrier = pltpu.get_barrier_semaphore()

    @pl.loop(1, devices)
    def _(j):
        to = (me + j) % devices
        pl.semaphore_signal(
            barrier, inc=1, device_id=(to // heads, to % heads), device_id_type=MESH
        )

    lane = lax.broadcasted_iota(jnp.int32, (8, 128), 1)
    block = jnp.where(lane < chips, 2 * lane, 2 * (lane - chips) + 1)
    block = jnp.where(lane < 2 * chips, block, -9)
    mine = s * heads + h
    entries = [mine - 1, mine, mine + 1]
    entries += [global_ref[e] for e in range(GLOB)]
    entries += [random_ref[h, e] for e in range(RAND)]
    count = jnp.zeros((8, 128), jnp.float32)
    for entry in entries:
        count = count + jnp.where(block == entry, 1.0, 0.0)
    cb[place] = count

    pl.semaphore_wait(barrier, devices - 1)

    def columns(to_s, to_x):
        return pl.ds(pl.multiple_of((seq * to_x + to_s) * HEAD_SIZE, HEAD_SIZE), HEAD_SIZE)

    def block_copy(a, j):
        to = (place + j) % chips
        to_s, to_x = to // planes, to % planes
        if a < 4:
            src, dst = sources[a].at[:, columns(to_s, to_x)], landing[a].at[place]
        else:
            src, dst = cb.at[place], cb.at[place]
        return pltpu.make_async_remote_copy(
            src_ref=src, dst_ref=dst, send_sem=send_sem.at[a, j], recv_sem=recv_sem.at[a, place],
            device_id=(to_s, 2 * to_x + c), device_id_type=MESH,
        )

    def arrival(a, p):
        ref = landing[a].at[p] if a < 4 else cb.at[p]
        return pltpu.make_async_remote_copy(
            src_ref=ref, dst_ref=ref, send_sem=send_sem.at[a, 0], recv_sem=recv_sem.at[a, p],
            device_id=sibling, device_id_type=MESH,
        )

    own = [
        pltpu.make_async_copy(
            sources[a].at[:, columns(s, x)], landing[a].at[place], own_sem.at[a]
        )
        for a in range(4)
    ]
    for a in range(4):
        own[a].start()
    for group in ((0, 4, 1), (2, 3)):
        @pl.loop(1, chips)
        def _(j):
            for a in group:
                block_copy(a, j).start()
    for a in range(4):
        own[a].wait()

    def swap(n, part):
        ref = (kb, vb)[n].at[part]
        return pltpu.make_async_remote_copy(
            src_ref=ref, dst_ref=ref, send_sem=swap_send.at[n], recv_sem=swap_recv.at[n],
            device_id=sibling, device_id_type=MESH,
        )

    def arrive(a):
        @pl.loop(1, chips)
        def _(j):
            arrival(a, (place + j) % chips).wait_recv()

    arrive(0)
    swap(0, c).start()
    arrive(4)
    arrive(1)

    rows = lax.broadcasted_iota(jnp.int32, (8 * chips, chips * BLOCK_TOKENS), 0)
    cols = lax.broadcasted_iota(jnp.int32, (8 * chips, chips * BLOCK_TOKENS), 1)
    spread = jnp.where(rows == 8 * (cols // BLOCK_TOKENS), 1.0, 0.0)
    counts = contract(cb[...].reshape(8 * chips, 128), spread, 0, 0)[: 2 * chips]
    logs = jnp.where(counts > 0.5, jnp.log(jnp.maximum(counts, 1.0)), NEG_FILL)
    width = GROUP * BLOCK_TOKENS
    for u in range(chips // GROUP):
        bias[u] = logs[:, u * width : (u + 1) * width]

    arrive(2)
    swap(1, c).start()
    arrive(3)
    dka[...] = jnp.zeros_like(dka)
    dva[...] = jnp.zeros_like(dva)
    swap(0, 1 - c).wait_recv()
    swap(1, 1 - c).wait_recv()

    total = 2 * chips * BLOCK_TOKENS
    scale = 1.0 / math.sqrt(HEAD_SIZE)

    @pl.loop(0, chips // GROUP)
    def _(u):
        picked = pl.ds(u * GROUP, GROUP)
        keys = kb[...].reshape(total, HEAD_SIZE)
        values = vb[...].reshape(total, HEAD_SIZE)
        query = qb[picked].reshape(width, HEAD_SIZE)
        cotan = gb[picked].reshape(width, HEAD_SIZE)
        score = contract(keys, query, 1, 1).reshape(2 * chips, BLOCK_TOKENS, width)
        score = (score * scale + bias[u][:, None, :]).reshape(total, width)
        power = jnp.exp(score - jnp.max(score, axis=0, keepdims=True))
        prob = power * (1.0 / jnp.sum(power, axis=0, keepdims=True))
        low = prob.astype(jnp.bfloat16)
        dprob = contract(values, cotan, 1, 1)
        delta = jnp.sum(prob * dprob, axis=0, keepdims=True)
        dscore = (prob * (dprob - delta) * scale).astype(jnp.bfloat16)
        attended = contract(low, values, 0, 0)
        dquery = contract(dscore, keys, 0, 0)
        halves = (GROUP // planes, planes, BLOCK_TOKENS, HEAD_SIZE)
        slot = pl.ds(u * (GROUP // planes), GROUP // planes)
        stage[0, slot] = attended.astype(jnp.bfloat16).reshape(halves)
        stage[1, slot] = dquery.astype(jnp.bfloat16).reshape(halves)
        dka[...] += contract(dscore, query, 1, 0).reshape(dka.shape)
        dva[...] += contract(low, cotan, 1, 0).reshape(dva.shape)

    def grad_copy(n):
        return pltpu.make_async_remote_copy(
            src_ref=(dka, dva)[n].at[1 - c], dst_ref=(dkr, dvr)[n],
            send_sem=grad_send.at[n], recv_sem=grad_recv.at[n],
            device_id=sibling, device_id_type=MESH,
        )

    grad_copy(0).start()
    grad_copy(1).start()

    results = (out_ref, dq_ref, dk_ref, dv_ref)
    out_core, out_slot = s // per_out, s % per_out

    def out_copy(a, t):
        lanes = pl.ds(pl.multiple_of(out_slot * HEAD_SIZE, HEAD_SIZE), HEAD_SIZE)
        return pltpu.make_async_remote_copy(
            src_ref=stage.at[a, t], dst_ref=results[a].at[:, c, :, lanes],
            send_sem=out_send.at[a, t], recv_sem=out_recv.at[a, out_slot, c],
            device_id=(t, 2 * x + out_core), device_id_type=MESH,
        )

    def out_own(a):
        lanes = pl.ds(pl.multiple_of(out_slot * HEAD_SIZE, HEAD_SIZE), HEAD_SIZE)
        return pltpu.make_async_copy(
            stage.at[a, s], results[a].at[:, c, :, lanes], own_sem.at[a]
        )

    keep = out_core == c

    def send_out(a):
        @pl.loop(1, seq)
        def _(j):
            out_copy(a, (s + j) % seq).start()

        @pl.when(keep)
        def _():
            out_own(a).start()

        @pl.when(jnp.logical_not(keep))
        def _():
            out_copy(a, s).start()

    send_out(0)
    send_out(1)
    for n in range(2):
        grad_copy(n).wait_recv()
        final = (dka, dva)[n][c] + (dkr, dvr)[n][...]
        stage[2 + n] = final.astype(jnp.bfloat16).reshape(stage.shape[1:])
        send_out(2 + n)

    for a in range(5):
        @pl.loop(1, chips)
        def _(j):
            block_copy(a, j).wait_send()
    for n in range(2):
        swap(n, c).wait_send()
        grad_copy(n).wait_send()
    for a in range(4):
        @pl.loop(1, seq)
        def _(j):
            out_copy(a, (s + j) % seq).wait_send()

        @pl.when(keep)
        def _():
            out_own(a).wait()

        @pl.when(jnp.logical_not(keep))
        def _():
            out_copy(a, s).wait_send()

        for d in range(per_out):
            for core in range(2):
                @pl.when(jnp.logical_not((s == c * per_out + d) & (core == c)))
                def _():
                    lanes = pl.ds(d * HEAD_SIZE, HEAD_SIZE)
                    ref = results[a].at[:, core, :, lanes]
                    pltpu.make_async_remote_copy(
                        src_ref=stage.at[a, 0], dst_ref=ref, send_sem=out_send.at[a, 0],
                        recv_sem=out_recv.at[a, d, core],
                        device_id=sibling, device_id_type=MESH,
                    ).wait_recv()


def by_head(seq, heads, queries, keys, values, cotangent, random_blocks, global_blocks):
    rows, feat = queries.shape
    planes = heads // 2
    chips = seq * planes
    per_out = feat // HEAD_SIZE // heads
    half = chips * rows
    low, wide = jnp.bfloat16, jnp.float32
    dma = pltpu.SemaphoreType.DMA
    shape = jax.ShapeDtypeStruct((planes, 2, rows, per_out * HEAD_SIZE), low)
    blocks = (chips, rows, HEAD_SIZE)
    flops = 6 * 2 * half * 2 * half * HEAD_SIZE
    results = pl.pallas_call(
        functools.partial(head_kernel, seq, heads, per_out),
        out_shape=[shape] * 4,
        in_specs=[pl.BlockSpec(memory_space=pl.ANY)] * 4
        + [pl.BlockSpec(memory_space=pltpu.SMEM)] * 2,
        out_specs=[pl.BlockSpec(memory_space=pl.ANY)] * 4,
        scratch_shapes=[
            pltpu.VMEM((2,) + blocks, low),
            pltpu.VMEM(blocks, low),
            pltpu.VMEM((2,) + blocks, low),
            pltpu.VMEM(blocks, low),
            pltpu.VMEM((chips, 8, 128), wide),
            pltpu.VMEM((chips // GROUP, 2 * chips, GROUP * rows), wide),
            pltpu.VMEM((2, half, HEAD_SIZE), wide),
            pltpu.VMEM((2, half, HEAD_SIZE), wide),
            pltpu.VMEM((half, HEAD_SIZE), wide),
            pltpu.VMEM((half, HEAD_SIZE), wide),
            pltpu.VMEM((4, seq, planes, rows, HEAD_SIZE), low),
            dma((5, chips)),
            dma((5, chips)),
            dma((4,)),
            dma((2,)),
            dma((2,)),
            dma((2,)),
            dma((2,)),
            dma((4, seq)),
            dma((4, per_out, 2)),
        ],
        compiler_params=pltpu.CompilerParams(
            collective_id=0, has_side_effects=True, vmem_limit_bytes=48 * 2**20
        ),
        cost_estimate=pl.CostEstimate(
            flops=flops, bytes_accessed=16 * rows * feat, transcendentals=2 * half * half
        ),
    )(keys, queries, values, cotangent, random_blocks, global_blocks)
    return tuple(r.reshape(2 * planes * rows, per_out * HEAD_SIZE) for r in results)


def shards_or_heads(queries, keys, values, cotangent, random_blocks, global_blocks):
    seq, heads = lax.axis_size("seq"), lax.axis_size("head")
    rows, feat = queries.shape
    count = feat // HEAD_SIZE
    one_each = heads == 4 and 2 * count == seq * heads and rows == BLOCK_TOKENS
    args = (queries, keys, values, cotangent, random_blocks, global_blocks)
    if one_each and seq == 2 * (count // heads):
        return by_head(seq, heads, *args)
    return shards(*args)


def solution(mesh):
    in_specs = (
        P(("seq", "head"), None),
        P(("seq", "head"), None),
        P(("seq", "head"), None),
        P(("seq", "head"), None),
        P("seq", None),
        P(),
    )
    out_specs = (P("seq", "head"), P("seq", "head"), P("seq", "head"), P("seq", "head"))
    return jax.shard_map(
        shards_or_heads, mesh=mesh, in_specs=in_specs, out_specs=out_specs, check_vma=False
    )
```

```python
import functools
import math

import jax
import jax.numpy as jnp
from jax import lax
from jax.experimental import pallas as pl
from jax.experimental.pallas import tpu as pltpu
from jax.sharding import PartitionSpec as P

HEAD_SIZE = 128
BLOCK_TOKENS = 64
GLOB = 2
RAND = 3


NEG_FILL = -1e30


def padded(shard, sides, width):
    for axis, dim in sides:
        size, length = (lax.axis_size(axis), shard.shape[dim])
        up = [(i, (i + 1) % size) for i in range(size - 1)]
        down = [(j, i) for i, j in up]
        last = lax.slice_in_dim(shard, length - width, length, axis=dim)
        leading = lax.slice_in_dim(shard, 0, width, axis=dim)
        before = lax.ppermute(last, axis, up)
        after = lax.ppermute(leading, axis, down)
        shard = jnp.concatenate([before, shard, after], axis=dim)
    return shard


def broadcast(block, axis, source):
    block = jnp.where(lax.axis_index(axis) == source, block, jnp.zeros_like(block))
    return lax.psum(block, axis)


def entry_ranks(owner_ids):
    count = owner_ids.shape[-1]
    earlier = jnp.arange(count)[None, :] < jnp.arange(count)[:, None]
    same_owner = owner_ids[..., :, None] == owner_ids[..., None, :]
    return jnp.sum((same_owner & earlier).astype(jnp.int32), axis=-1)


def spread_band(band_part):
    return (
        jnp.pad(band_part[:, 0], ((0, 2), (0, 0), (0, 0)))
        + jnp.pad(band_part[:, 1], ((1, 1), (0, 0), (0, 0)))
        + jnp.pad(band_part[:, 2], ((2, 0), (0, 0), (0, 0)))
    )


def shards(queries, keys, values, cotangent, random_blocks, global_blocks):
    query_rows, gathered_keys, gathered_values, cotan_rows = (
        lax.all_to_all(queries, "head", split_axis=1, concat_axis=0, tiled=True),
        lax.all_to_all(keys, "head", split_axis=1, concat_axis=0, tiled=True),
        lax.all_to_all(values, "head", split_axis=1, concat_axis=0, tiled=True),
        lax.all_to_all(cotangent, "head", split_axis=1, concat_axis=0, tiled=True),
    )
    row_count, width = query_rows.shape
    head_count = width // HEAD_SIZE
    block_count = row_count // BLOCK_TOKENS
    shard_count = lax.axis_size("seq")
    my_index = lax.axis_index("seq")
    entry_count = block_count * RAND
    slot_cap = (3 * entry_count + 2 * shard_count - 1) // (2 * shard_count)
    slot_count = shard_count * slot_cap
    key_block_sets = 3 + GLOB + RAND
    logit_scale = 1.0 / math.sqrt(HEAD_SIZE)
    key_value = jnp.stack([gathered_keys, gathered_values])
    widened = padded(key_value, (("seq", 1),), BLOCK_TOKENS)
    widened = widened.reshape(2, block_count + 2, BLOCK_TOKENS, width)
    band_rows = jnp.stack([widened[:, :-2], widened[:, 1:-1], widened[:, 2:]], axis=2)
    own_blocks = key_value.reshape(2, block_count, BLOCK_TOKENS, width)
    owner_global = global_blocks // block_count
    local_global = global_blocks % block_count
    fetched = []
    for number in range(GLOB):
        mine = jnp.take(own_blocks, local_global[number], axis=1)
        fetched.append(broadcast(mine, "seq", owner_global[number]))
    global_rows = jnp.stack(fetched, axis=1)
    entry_ids = random_blocks.reshape(entry_count)
    owner_ids = entry_ids // block_count
    slot_ids = owner_ids * slot_cap + entry_ranks(owner_ids)
    slot_hits = slot_ids[None, :] == jnp.arange(slot_count)[:, None]
    filled = jnp.any(slot_hits, axis=1)
    source = jnp.sum(jnp.where(slot_hits, jnp.arange(entry_count)[None, :], 0), axis=1)
    wanted = jnp.sum(jnp.where(slot_hits, (entry_ids % block_count)[None, :], 0), axis=1)
    asked_ids = lax.all_to_all(wanted, "seq", split_axis=0, concat_axis=0, tiled=True)
    outgoing = jnp.take(own_blocks, asked_ids, axis=1)
    incoming = lax.all_to_all(outgoing, "seq", split_axis=1, concat_axis=1, tiled=True)
    random_rows = jnp.take(incoming, slot_ids, axis=1).reshape(
        2, block_count, RAND, BLOCK_TOKENS, width
    )

    def assemble_keys(which):
        spread_global = jnp.broadcast_to(
            global_rows[which][None], (block_count, GLOB, BLOCK_TOKENS, width)
        )
        joined = jnp.concatenate([band_rows[which], spread_global, random_rows[which]], axis=1)
        return joined.reshape(block_count, key_block_sets * BLOCK_TOKENS, head_count, HEAD_SIZE)

    key_all = assemble_keys(0)
    value_all = assemble_keys(1)
    block_number = my_index * block_count + jnp.arange(block_count)
    total_blocks = shard_count * block_count
    always = jnp.ones((block_count,), dtype=bool)
    group_ok = jnp.stack(
        [block_number >= 1, always, block_number <= total_blocks - 2] + [always] * (GLOB + RAND),
        axis=1,
    )
    valid_keys = jnp.repeat(group_ok, BLOCK_TOKENS, axis=1)[:, None, None, :]
    query_blocks = query_rows.reshape(block_count, BLOCK_TOKENS, head_count, HEAD_SIZE)
    cotan_blocks = cotan_rows.reshape(block_count, BLOCK_TOKENS, head_count, HEAD_SIZE)
    score_matrix = (
        jnp.einsum("bqhd,bkhd->bhqk", query_blocks, key_all, preferred_element_type=jnp.float32)
        * logit_scale
    )
    score_matrix = jnp.where(valid_keys, score_matrix, NEG_FILL)
    row_peak = jnp.max(score_matrix, axis=-1, keepdims=True)
    exponent = jnp.exp(score_matrix - row_peak)
    weights = exponent / jnp.sum(exponent, axis=-1, keepdims=True)
    weights_low = weights.astype(jnp.bfloat16)
    attended_output = jnp.einsum(
        "bhqk,bkhd->bqhd", weights_low, value_all, preferred_element_type=jnp.float32
    ).astype(jnp.bfloat16)
    weight_gradient = jnp.einsum(
        "bqhd,bkhd->bhqk", cotan_blocks, value_all, preferred_element_type=jnp.float32
    )
    row_delta = jnp.sum(weights * weight_gradient, axis=-1, keepdims=True)
    score_grad = (weights * (weight_gradient - row_delta) * logit_scale).astype(jnp.bfloat16)
    query_gradient = jnp.einsum(
        "bhqk,bkhd->bqhd", score_grad, key_all, preferred_element_type=jnp.float32
    ).astype(jnp.bfloat16)

    def part_grads(first, count):
        low_key = first * BLOCK_TOKENS
        high_key = (first + count) * BLOCK_TOKENS
        key_part = jnp.einsum(
            "bhqk,bqhd->bkhd",
            score_grad[..., low_key:high_key],
            query_blocks,
            preferred_element_type=jnp.float32,
        )
        value_part = jnp.einsum(
            "bhqk,bqhd->bkhd",
            weights_low[..., low_key:high_key],
            cotan_blocks,
            preferred_element_type=jnp.float32,
        )
        return (
            key_part.reshape(block_count, count, BLOCK_TOKENS, width),
            value_part.reshape(block_count, count, BLOCK_TOKENS, width),
        )

    band_key, band_value = part_grads(0, 3)
    extended_key = spread_band(band_key)
    extended_value = spread_band(band_value)
    rim_pair = jnp.stack(
        [
            jnp.stack([extended_key[0], extended_key[-1]]),
            jnp.stack([extended_value[0], extended_value[-1]]),
        ]
    )
    rimmed = padded(rim_pair.astype(jnp.bfloat16), (("seq", 1),), 1).astype(rim_pair.dtype)
    key_local = extended_key[1:-1].at[0].add(rimmed[0, 0]).at[-1].add(rimmed[0, 3])
    value_local = extended_value[1:-1].at[0].add(rimmed[1, 0]).at[-1].add(rimmed[1, 3])
    global_key, global_value = part_grads(3, GLOB)
    total_key, total_value = lax.psum(
        (jnp.sum(global_key, axis=0), jnp.sum(global_value, axis=0)), "seq"
    )
    for number in range(GLOB):
        owned = owner_global[number] == my_index
        key_local = key_local.at[local_global[number]].add(jnp.where(owned, total_key[number], 0.0))
        value_local = value_local.at[local_global[number]].add(
            jnp.where(owned, total_value[number], 0.0)
        )
    random_key, random_value = part_grads(3 + GLOB, RAND)
    keep = filled[:, None, None]
    send_key = jnp.where(
        keep, jnp.take(random_key.reshape(entry_count, BLOCK_TOKENS, width), source, axis=0), 0.0
    ).astype(jnp.bfloat16)
    send_value = jnp.where(
        keep, jnp.take(random_value.reshape(entry_count, BLOCK_TOKENS, width), source, axis=0), 0.0
    ).astype(jnp.bfloat16)
    arrived_key, arrived_value = (
        lax.all_to_all(send_key, "seq", split_axis=0, concat_axis=0, tiled=True),
        lax.all_to_all(send_value, "seq", split_axis=0, concat_axis=0, tiled=True),
    )
    owner_hits = (asked_ids[None, :] == jnp.arange(block_count)[:, None]).astype(jnp.float32)
    key_local = key_local + jnp.einsum(
        "js,srf->jrf", owner_hits, arrived_key.astype(jnp.float32), precision=lax.Precision.HIGHEST
    )
    value_local = value_local + jnp.einsum(
        "js,srf->jrf",
        owner_hits,
        arrived_value.astype(jnp.float32),
        precision=lax.Precision.HIGHEST,
    )
    return (
        attended_output.reshape(row_count, width),
        query_gradient.reshape(row_count, width),
        key_local.reshape(row_count, width).astype(jnp.bfloat16),
        value_local.reshape(row_count, width).astype(jnp.bfloat16),
    )


MESH = pl.DeviceIdType.MESH
GROUP = 4


def contract(a, b, dim_a, dim_b):
    return lax.dot_general(
        a, b, (((dim_a,), (dim_b,)), ((), ())), preferred_element_type=jnp.float32
    )


def head_kernel(
    seq, heads, per_out,
    k_ref, q_ref, v_ref, g_ref, random_ref, global_ref,
    out_ref, dq_ref, dk_ref, dv_ref,
    kb, qb, vb, gb, cb, bias, probs, dka, dva, dkr, dvr, stage,
    send_sem, recv_sem, own_sem, swap_send, swap_recv, grad_send, grad_recv,
    out_send, out_recv,
):
    s = lax.axis_index("seq")
    h = lax.axis_index("head")
    x, c = h // 2, h % 2
    planes = heads // 2
    chips = seq * planes
    devices = seq * heads
    me = s * heads + h
    place = s * planes + x
    sources = (k_ref, q_ref, v_ref, g_ref)
    landing = (kb.at[c], qb, vb.at[c], gb)
    sibling = (s, 2 * x + 1 - c)

    barrier = pltpu.get_barrier_semaphore()

    @pl.loop(1, devices)
    def _(j):
        to = (me + j) % devices
        pl.semaphore_signal(
            barrier, inc=1, device_id=(to // heads, to % heads), device_id_type=MESH
        )

    lane = lax.broadcasted_iota(jnp.int32, (8, 128), 1)
    block = jnp.where(lane < chips, 2 * lane, 2 * (lane - chips) + 1)
    block = jnp.where(lane < 2 * chips, block, -9)
    mine = s * heads + h
    entries = [mine - 1, mine, mine + 1]
    entries += [global_ref[e] for e in range(GLOB)]
    entries += [random_ref[h, e] for e in range(RAND)]
    count = jnp.zeros((8, 128), jnp.float32)
    for entry in entries:
        count = count + jnp.where(block == entry, 1.0, 0.0)
    cb[place] = count

    pl.semaphore_wait(barrier, devices - 1)

    def columns(to_s, to_x):
        return pl.ds(pl.multiple_of((seq * to_x + to_s) * HEAD_SIZE, HEAD_SIZE), HEAD_SIZE)

    def block_copy(a, j):
        to = (place + j) % chips
        to_s, to_x = to // planes, to % planes
        if a < 4:
            src, dst = sources[a].at[:, columns(to_s, to_x)], landing[a].at[place]
        else:
            src, dst = cb.at[place], cb.at[place]
        return pltpu.make_async_remote_copy(
            src_ref=src, dst_ref=dst, send_sem=send_sem.at[a, j], recv_sem=recv_sem.at[a, place],
            device_id=(to_s, 2 * to_x + c), device_id_type=MESH,
        )

    def arrival(a, p):
        ref = landing[a].at[p] if a < 4 else cb.at[p]
        return pltpu.make_async_remote_copy(
            src_ref=ref, dst_ref=ref, send_sem=send_sem.at[a, 0], recv_sem=recv_sem.at[a, p],
            device_id=sibling, device_id_type=MESH,
        )

    own = [
        pltpu.make_async_copy(
            sources[a].at[:, columns(s, x)], landing[a].at[place], own_sem.at[a]
        )
        for a in range(4)
    ]
    for a in range(4):
        own[a].start()
    parts = chips // GROUP
    part = place // GROUP

    for group in ((0, 4), (1,), (3,), (2,)):
        for first, last in ((chips // 2, chips), (1, chips // 2)):
            @pl.loop(first, last)
            def _(j):
                for a in group:
                    block_copy(a, j).start()
    for a in range(4):
        own[a].wait()

    def swap(n, core, m):
        ref = (kb, vb)[n].at[core, pl.ds(m * GROUP, GROUP)]
        return pltpu.make_async_remote_copy(
            src_ref=ref, dst_ref=ref, send_sem=swap_send.at[n, m], recv_sem=swap_recv.at[n, m],
            device_id=sibling, device_id_type=MESH,
        )

    def arrive(a):
        @pl.loop(1, chips)
        def _(j):
            arrival(a, (place + j) % chips).wait_recv()

    def arrive_and_swap(a, n):
        @pl.loop(0, parts)
        def _(v):
            m = (part + parts // 2 + parts - v) % parts
            for d in range(GROUP):
                @pl.when(m * GROUP + d != place)
                def _():
                    arrival(a, m * GROUP + d).wait_recv()

            swap(n, c, m).start()

    def swapped(n):
        @pl.loop(0, parts)
        def _(m):
            swap(n, 1 - c, m).wait_recv()

    arrive_and_swap(0, 0)
    arrive(4)

    rows = lax.broadcasted_iota(jnp.int32, (8 * chips, chips * BLOCK_TOKENS), 0)
    cols = lax.broadcasted_iota(jnp.int32, (8 * chips, chips * BLOCK_TOKENS), 1)
    spread = jnp.where(rows == 8 * (cols // BLOCK_TOKENS), 1.0, 0.0)
    counts = contract(cb[...].reshape(8 * chips, 128), spread, 0, 0)[: 2 * chips]
    logs = jnp.where(counts > 0.5, jnp.log(jnp.maximum(counts, 1.0)), NEG_FILL)
    width = GROUP * BLOCK_TOKENS
    for u in range(chips // GROUP):
        bias[u] = logs[:, u * width : (u + 1) * width]

    dka[...] = jnp.zeros_like(dka)
    dva[...] = jnp.zeros_like(dva)
    arrive(1)
    swapped(0)

    total = 2 * chips * BLOCK_TOKENS
    scale = 1.0 / math.sqrt(HEAD_SIZE)

    @pl.loop(0, parts)
    def _(u):
        keys = kb[...].reshape(total, HEAD_SIZE)
        query = qb[pl.ds(u * GROUP, GROUP)].reshape(width, HEAD_SIZE)
        score = contract(keys, query, 1, 1).reshape(2 * chips, BLOCK_TOKENS, width)
        score = (score * scale + bias[u][:, None, :]).reshape(total, width)
        power = jnp.exp(score - jnp.max(score, axis=0, keepdims=True))
        probs[u] = power * (1.0 / jnp.sum(power, axis=0, keepdims=True))

    arrive(3)

    @pl.loop(0, parts)
    def _(u):
        cotan = gb[pl.ds(u * GROUP, GROUP)].reshape(width, HEAD_SIZE)
        low = probs[u].astype(jnp.bfloat16)
        dva[...] += contract(low, cotan, 1, 0).reshape(dva.shape)

    def grad_copy(n):
        return pltpu.make_async_remote_copy(
            src_ref=(dka, dva)[n].at[1 - c], dst_ref=(dkr, dvr)[n],
            send_sem=grad_send.at[n], recv_sem=grad_recv.at[n],
            device_id=sibling, device_id_type=MESH,
        )

    grad_copy(1).start()

    results = (out_ref, dq_ref, dk_ref, dv_ref)
    out_core, out_slot = s // per_out, s % per_out

    def out_copy(a, t):
        lanes = pl.ds(pl.multiple_of(out_slot * HEAD_SIZE, HEAD_SIZE), HEAD_SIZE)
        return pltpu.make_async_remote_copy(
            src_ref=stage.at[a, t], dst_ref=results[a].at[:, c, :, lanes],
            send_sem=out_send.at[a, t], recv_sem=out_recv.at[a, out_slot, c],
            device_id=(t, 2 * x + out_core), device_id_type=MESH,
        )

    def out_own(a):
        lanes = pl.ds(pl.multiple_of(out_slot * HEAD_SIZE, HEAD_SIZE), HEAD_SIZE)
        return pltpu.make_async_copy(
            stage.at[a, s], results[a].at[:, c, :, lanes], own_sem.at[a]
        )

    def stays(t):
        return (out_core == c) & (t == s)

    def send_out(a, t):
        @pl.when(stays(t))
        def _():
            out_own(a).start()

        @pl.when(jnp.logical_not(stays(t)))
        def _():
            out_copy(a, t).start()

    def send_grad(n):
        grad_copy(n).wait_recv()
        final = (dka, dva)[n][c] + (dkr, dvr)[n][...]
        stage[2 + n] = final.astype(jnp.bfloat16).reshape(stage.shape[1:])

        @pl.loop(0, seq)
        def _(j):
            send_out(2 + n, (s + seq // 2 + j) % seq)

    arrive_and_swap(2, 1)
    send_grad(1)
    swapped(1)
    shards_each = GROUP // planes

    @pl.loop(0, parts)
    def _(v):
        u = (part + parts // 2 + v) % parts
        keys = kb[...].reshape(total, HEAD_SIZE)
        values = vb[...].reshape(total, HEAD_SIZE)
        query = qb[pl.ds(u * GROUP, GROUP)].reshape(width, HEAD_SIZE)
        cotan = gb[pl.ds(u * GROUP, GROUP)].reshape(width, HEAD_SIZE)
        prob = probs[u]
        halves = (shards_each, planes, BLOCK_TOKENS, HEAD_SIZE)
        slot = pl.ds(u * shards_each, shards_each)
        attended = contract(prob.astype(jnp.bfloat16), values, 0, 0)
        stage[0, slot] = attended.astype(jnp.bfloat16).reshape(halves)
        for d in range(shards_each):
            send_out(0, u * shards_each + d)
        dprob = contract(values, cotan, 1, 1)
        delta = jnp.sum(prob * dprob, axis=0, keepdims=True)
        dscore = (prob * (dprob - delta) * scale).astype(jnp.bfloat16)
        dquery = contract(dscore, keys, 0, 0)
        stage[1, slot] = dquery.astype(jnp.bfloat16).reshape(halves)
        for d in range(shards_each):
            send_out(1, u * shards_each + d)
        dka[...] += contract(dscore, query, 1, 0).reshape(dka.shape)

    grad_copy(0).start()
    send_grad(0)

    for a in range(5):
        @pl.loop(1, chips)
        def _(j):
            block_copy(a, j).wait_send()
    for n in range(2):
        @pl.loop(0, parts)
        def _(m):
            swap(n, c, m).wait_send()

        grad_copy(n).wait_send()
    for a in range(4):
        @pl.loop(0, seq)
        def _(t):
            @pl.when(stays(t))
            def _():
                out_own(a).wait()

            @pl.when(jnp.logical_not(stays(t)))
            def _():
                out_copy(a, t).wait_send()

        for d in range(per_out):
            for core in range(2):
                @pl.when(jnp.logical_not((s == c * per_out + d) & (core == c)))
                def _():
                    lanes = pl.ds(d * HEAD_SIZE, HEAD_SIZE)
                    ref = results[a].at[:, core, :, lanes]
                    pltpu.make_async_remote_copy(
                        src_ref=stage.at[a, 0], dst_ref=ref, send_sem=out_send.at[a, 0],
                        recv_sem=out_recv.at[a, d, core],
                        device_id=sibling, device_id_type=MESH,
                    ).wait_recv()


def by_head(seq, heads, queries, keys, values, cotangent, random_blocks, global_blocks):
    rows, feat = queries.shape
    planes = heads // 2
    chips = seq * planes
    per_out = feat // HEAD_SIZE // heads
    half = chips * rows
    low, wide = jnp.bfloat16, jnp.float32
    dma = pltpu.SemaphoreType.DMA
    shape = jax.ShapeDtypeStruct((planes, 2, rows, per_out * HEAD_SIZE), low)
    blocks = (chips, rows, HEAD_SIZE)
    flops = 6 * 2 * half * 2 * half * HEAD_SIZE
    results = pl.pallas_call(
        functools.partial(head_kernel, seq, heads, per_out),
        out_shape=[shape] * 4,
        in_specs=[pl.BlockSpec(memory_space=pl.ANY)] * 4
        + [pl.BlockSpec(memory_space=pltpu.SMEM)] * 2,
        out_specs=[pl.BlockSpec(memory_space=pl.ANY)] * 4,
        scratch_shapes=[
            pltpu.VMEM((2,) + blocks, low),
            pltpu.VMEM(blocks, low),
            pltpu.VMEM((2,) + blocks, low),
            pltpu.VMEM(blocks, low),
            pltpu.VMEM((chips, 8, 128), wide),
            pltpu.VMEM((chips // GROUP, 2 * chips, GROUP * rows), wide),
            pltpu.VMEM((chips // GROUP, 2 * half, GROUP * rows), wide),
            pltpu.VMEM((2, half, HEAD_SIZE), wide),
            pltpu.VMEM((2, half, HEAD_SIZE), wide),
            pltpu.VMEM((half, HEAD_SIZE), wide),
            pltpu.VMEM((half, HEAD_SIZE), wide),
            pltpu.VMEM((4, seq, planes, rows, HEAD_SIZE), low),
            dma((5, chips)),
            dma((5, chips)),
            dma((4,)),
            dma((2, chips // GROUP)),
            dma((2, chips // GROUP)),
            dma((2,)),
            dma((2,)),
            dma((4, seq)),
            dma((4, per_out, 2)),
        ],
        compiler_params=pltpu.CompilerParams(
            collective_id=0, has_side_effects=True, vmem_limit_bytes=63 * 2**20
        ),
        cost_estimate=pl.CostEstimate(
            flops=flops, bytes_accessed=16 * rows * feat, transcendentals=2 * half * half
        ),
    )(keys, queries, values, cotangent, random_blocks, global_blocks)
    return tuple(r.reshape(2 * planes * rows, per_out * HEAD_SIZE) for r in results)


def shards_or_heads(queries, keys, values, cotangent, random_blocks, global_blocks):
    seq, heads = lax.axis_size("seq"), lax.axis_size("head")
    rows, feat = queries.shape
    count = feat // HEAD_SIZE
    one_each = heads == 4 and 2 * count == seq * heads and rows == BLOCK_TOKENS
    args = (queries, keys, values, cotangent, random_blocks, global_blocks)
    if one_each and seq == 2 * (count // heads):
        return by_head(seq, heads, *args)
    return shards(*args)


def solution(mesh):
    in_specs = (
        P(("seq", "head"), None),
        P(("seq", "head"), None),
        P(("seq", "head"), None),
        P(("seq", "head"), None),
        P("seq", None),
        P(),
    )
    out_specs = (P("seq", "head"), P("seq", "head"), P("seq", "head"), P("seq", "head"))
    return jax.shard_map(
        shards_or_heads, mesh=mesh, in_specs=in_specs, out_specs=out_specs, check_vma=False
    )
```

```python
import functools
import math

import jax
import jax.numpy as jnp
from jax import lax
from jax.experimental import pallas as pl
from jax.experimental.pallas import tpu as pltpu
from jax.sharding import PartitionSpec as P

HEAD_SIZE = 128
BLOCK_TOKENS = 64
GLOB = 2
RAND = 3


NEG_FILL = -1e30


def padded(shard, sides, width):
    for axis, dim in sides:
        size, length = (lax.axis_size(axis), shard.shape[dim])
        up = [(i, (i + 1) % size) for i in range(size - 1)]
        down = [(j, i) for i, j in up]
        last = lax.slice_in_dim(shard, length - width, length, axis=dim)
        leading = lax.slice_in_dim(shard, 0, width, axis=dim)
        before = lax.ppermute(last, axis, up)
        after = lax.ppermute(leading, axis, down)
        shard = jnp.concatenate([before, shard, after], axis=dim)
    return shard


def broadcast(block, axis, source):
    block = jnp.where(lax.axis_index(axis) == source, block, jnp.zeros_like(block))
    return lax.psum(block, axis)


def entry_ranks(owner_ids):
    count = owner_ids.shape[-1]
    earlier = jnp.arange(count)[None, :] < jnp.arange(count)[:, None]
    same_owner = owner_ids[..., :, None] == owner_ids[..., None, :]
    return jnp.sum((same_owner & earlier).astype(jnp.int32), axis=-1)


def spread_band(band_part):
    return (
        jnp.pad(band_part[:, 0], ((0, 2), (0, 0), (0, 0)))
        + jnp.pad(band_part[:, 1], ((1, 1), (0, 0), (0, 0)))
        + jnp.pad(band_part[:, 2], ((2, 0), (0, 0), (0, 0)))
    )


def shards(queries, keys, values, cotangent, random_blocks, global_blocks):
    query_rows, gathered_keys, gathered_values, cotan_rows = (
        lax.all_to_all(queries, "head", split_axis=1, concat_axis=0, tiled=True),
        lax.all_to_all(keys, "head", split_axis=1, concat_axis=0, tiled=True),
        lax.all_to_all(values, "head", split_axis=1, concat_axis=0, tiled=True),
        lax.all_to_all(cotangent, "head", split_axis=1, concat_axis=0, tiled=True),
    )
    row_count, width = query_rows.shape
    head_count = width // HEAD_SIZE
    block_count = row_count // BLOCK_TOKENS
    shard_count = lax.axis_size("seq")
    my_index = lax.axis_index("seq")
    entry_count = block_count * RAND
    slot_cap = (3 * entry_count + 2 * shard_count - 1) // (2 * shard_count)
    slot_count = shard_count * slot_cap
    key_block_sets = 3 + GLOB + RAND
    logit_scale = 1.0 / math.sqrt(HEAD_SIZE)
    key_value = jnp.stack([gathered_keys, gathered_values])
    widened = padded(key_value, (("seq", 1),), BLOCK_TOKENS)
    widened = widened.reshape(2, block_count + 2, BLOCK_TOKENS, width)
    band_rows = jnp.stack([widened[:, :-2], widened[:, 1:-1], widened[:, 2:]], axis=2)
    own_blocks = key_value.reshape(2, block_count, BLOCK_TOKENS, width)
    owner_global = global_blocks // block_count
    local_global = global_blocks % block_count
    fetched = []
    for number in range(GLOB):
        mine = jnp.take(own_blocks, local_global[number], axis=1)
        fetched.append(broadcast(mine, "seq", owner_global[number]))
    global_rows = jnp.stack(fetched, axis=1)
    entry_ids = random_blocks.reshape(entry_count)
    owner_ids = entry_ids // block_count
    slot_ids = owner_ids * slot_cap + entry_ranks(owner_ids)
    slot_hits = slot_ids[None, :] == jnp.arange(slot_count)[:, None]
    filled = jnp.any(slot_hits, axis=1)
    source = jnp.sum(jnp.where(slot_hits, jnp.arange(entry_count)[None, :], 0), axis=1)
    wanted = jnp.sum(jnp.where(slot_hits, (entry_ids % block_count)[None, :], 0), axis=1)
    asked_ids = lax.all_to_all(wanted, "seq", split_axis=0, concat_axis=0, tiled=True)
    outgoing = jnp.take(own_blocks, asked_ids, axis=1)
    incoming = lax.all_to_all(outgoing, "seq", split_axis=1, concat_axis=1, tiled=True)
    random_rows = jnp.take(incoming, slot_ids, axis=1).reshape(
        2, block_count, RAND, BLOCK_TOKENS, width
    )

    def assemble_keys(which):
        spread_global = jnp.broadcast_to(
            global_rows[which][None], (block_count, GLOB, BLOCK_TOKENS, width)
        )
        joined = jnp.concatenate([band_rows[which], spread_global, random_rows[which]], axis=1)
        return joined.reshape(block_count, key_block_sets * BLOCK_TOKENS, head_count, HEAD_SIZE)

    key_all = assemble_keys(0)
    value_all = assemble_keys(1)
    block_number = my_index * block_count + jnp.arange(block_count)
    total_blocks = shard_count * block_count
    always = jnp.ones((block_count,), dtype=bool)
    group_ok = jnp.stack(
        [block_number >= 1, always, block_number <= total_blocks - 2] + [always] * (GLOB + RAND),
        axis=1,
    )
    valid_keys = jnp.repeat(group_ok, BLOCK_TOKENS, axis=1)[:, None, None, :]
    query_blocks = query_rows.reshape(block_count, BLOCK_TOKENS, head_count, HEAD_SIZE)
    cotan_blocks = cotan_rows.reshape(block_count, BLOCK_TOKENS, head_count, HEAD_SIZE)
    score_matrix = (
        jnp.einsum("bqhd,bkhd->bhqk", query_blocks, key_all, preferred_element_type=jnp.float32)
        * logit_scale
    )
    score_matrix = jnp.where(valid_keys, score_matrix, NEG_FILL)
    row_peak = jnp.max(score_matrix, axis=-1, keepdims=True)
    exponent = jnp.exp(score_matrix - row_peak)
    weights = exponent / jnp.sum(exponent, axis=-1, keepdims=True)
    weights_low = weights.astype(jnp.bfloat16)
    attended_output = jnp.einsum(
        "bhqk,bkhd->bqhd", weights_low, value_all, preferred_element_type=jnp.float32
    ).astype(jnp.bfloat16)
    weight_gradient = jnp.einsum(
        "bqhd,bkhd->bhqk", cotan_blocks, value_all, preferred_element_type=jnp.float32
    )
    row_delta = jnp.sum(weights * weight_gradient, axis=-1, keepdims=True)
    score_grad = (weights * (weight_gradient - row_delta) * logit_scale).astype(jnp.bfloat16)
    query_gradient = jnp.einsum(
        "bhqk,bkhd->bqhd", score_grad, key_all, preferred_element_type=jnp.float32
    ).astype(jnp.bfloat16)

    def part_grads(first, count):
        low_key = first * BLOCK_TOKENS
        high_key = (first + count) * BLOCK_TOKENS
        key_part = jnp.einsum(
            "bhqk,bqhd->bkhd",
            score_grad[..., low_key:high_key],
            query_blocks,
            preferred_element_type=jnp.float32,
        )
        value_part = jnp.einsum(
            "bhqk,bqhd->bkhd",
            weights_low[..., low_key:high_key],
            cotan_blocks,
            preferred_element_type=jnp.float32,
        )
        return (
            key_part.reshape(block_count, count, BLOCK_TOKENS, width),
            value_part.reshape(block_count, count, BLOCK_TOKENS, width),
        )

    band_key, band_value = part_grads(0, 3)
    extended_key = spread_band(band_key)
    extended_value = spread_band(band_value)
    rim_pair = jnp.stack(
        [
            jnp.stack([extended_key[0], extended_key[-1]]),
            jnp.stack([extended_value[0], extended_value[-1]]),
        ]
    )
    rimmed = padded(rim_pair.astype(jnp.bfloat16), (("seq", 1),), 1).astype(rim_pair.dtype)
    key_local = extended_key[1:-1].at[0].add(rimmed[0, 0]).at[-1].add(rimmed[0, 3])
    value_local = extended_value[1:-1].at[0].add(rimmed[1, 0]).at[-1].add(rimmed[1, 3])
    global_key, global_value = part_grads(3, GLOB)
    total_key, total_value = lax.psum(
        (jnp.sum(global_key, axis=0), jnp.sum(global_value, axis=0)), "seq"
    )
    for number in range(GLOB):
        owned = owner_global[number] == my_index
        key_local = key_local.at[local_global[number]].add(jnp.where(owned, total_key[number], 0.0))
        value_local = value_local.at[local_global[number]].add(
            jnp.where(owned, total_value[number], 0.0)
        )
    random_key, random_value = part_grads(3 + GLOB, RAND)
    keep = filled[:, None, None]
    send_key = jnp.where(
        keep, jnp.take(random_key.reshape(entry_count, BLOCK_TOKENS, width), source, axis=0), 0.0
    ).astype(jnp.bfloat16)
    send_value = jnp.where(
        keep, jnp.take(random_value.reshape(entry_count, BLOCK_TOKENS, width), source, axis=0), 0.0
    ).astype(jnp.bfloat16)
    arrived_key, arrived_value = (
        lax.all_to_all(send_key, "seq", split_axis=0, concat_axis=0, tiled=True),
        lax.all_to_all(send_value, "seq", split_axis=0, concat_axis=0, tiled=True),
    )
    owner_hits = (asked_ids[None, :] == jnp.arange(block_count)[:, None]).astype(jnp.float32)
    key_local = key_local + jnp.einsum(
        "js,srf->jrf", owner_hits, arrived_key.astype(jnp.float32), precision=lax.Precision.HIGHEST
    )
    value_local = value_local + jnp.einsum(
        "js,srf->jrf",
        owner_hits,
        arrived_value.astype(jnp.float32),
        precision=lax.Precision.HIGHEST,
    )
    return (
        attended_output.reshape(row_count, width),
        query_gradient.reshape(row_count, width),
        key_local.reshape(row_count, width).astype(jnp.bfloat16),
        value_local.reshape(row_count, width).astype(jnp.bfloat16),
    )


MESH = pl.DeviceIdType.MESH
GROUP = 4


def contract(a, b, dim_a, dim_b):
    return lax.dot_general(
        a, b, (((dim_a,), (dim_b,)), ((), ())), preferred_element_type=jnp.float32
    )


def head_kernel(
    seq, heads, per_out,
    k_ref, q_ref, v_ref, g_ref, random_ref, global_ref,
    out_ref, dq_ref, dk_ref, dv_ref,
    kb, qb, vb, gb, cb, bias, probs, dka, dva, dkr, dvr, stage,
    kin, qin, vin, gin, send_sem, recv_sem, own_sem, swap_send, swap_recv, grad_send, grad_recv,
    out_send, out_recv,
):
    s = lax.axis_index("seq")
    h = lax.axis_index("head")
    x, c = h // 2, h % 2
    planes = heads // 2
    chips = seq * planes
    devices = seq * heads
    me = s * heads + h
    place = s * planes + x
    sources = (kin, qin, vin, gin)
    loads = [
        pltpu.make_async_copy(ref, sources[a], own_sem.at[a])
        for a, ref in enumerate((k_ref, q_ref, v_ref, g_ref))
    ]
    for load in loads:
        load.start()
    landing = (kb.at[c], qb, vb.at[c], gb)
    sibling = (s, 2 * x + 1 - c)

    barrier = pltpu.get_barrier_semaphore()

    @pl.loop(1, devices)
    def _(j):
        to = (me + j) % devices
        pl.semaphore_signal(
            barrier, inc=1, device_id=(to // heads, to % heads), device_id_type=MESH
        )

    lane = lax.broadcasted_iota(jnp.int32, (8, 128), 1)
    block = jnp.where(lane < chips, 2 * lane, 2 * (lane - chips) + 1)
    block = jnp.where(lane < 2 * chips, block, -9)
    mine = s * heads + h
    entries = [mine - 1, mine, mine + 1]
    entries += [global_ref[e] for e in range(GLOB)]
    entries += [random_ref[h, e] for e in range(RAND)]
    count = jnp.zeros((8, 128), jnp.float32)
    for entry in entries:
        count = count + jnp.where(block == entry, 1.0, 0.0)
    cb[place] = count

    for load in loads:
        load.wait()
    pl.semaphore_wait(barrier, devices - 1)

    def columns(to_s, to_x):
        return pl.ds(pl.multiple_of((seq * to_x + to_s) * HEAD_SIZE, HEAD_SIZE), HEAD_SIZE)

    def block_copy(a, j):
        to = (place + j) % chips
        to_s, to_x = to // planes, to % planes
        if a < 4:
            src, dst = sources[a].at[:, columns(to_s, to_x)], landing[a].at[place]
        else:
            src, dst = cb.at[place], cb.at[place]
        return pltpu.make_async_remote_copy(
            src_ref=src, dst_ref=dst, send_sem=send_sem.at[a, j], recv_sem=recv_sem.at[a, place],
            device_id=(to_s, 2 * to_x + c), device_id_type=MESH,
        )

    def arrival(a, p):
        ref = landing[a].at[p] if a < 4 else cb.at[p]
        return pltpu.make_async_remote_copy(
            src_ref=ref, dst_ref=ref, send_sem=send_sem.at[a, 0], recv_sem=recv_sem.at[a, p],
            device_id=sibling, device_id_type=MESH,
        )

    own = [
        pltpu.make_async_copy(
            sources[a].at[:, columns(s, x)], landing[a].at[place], own_sem.at[a]
        )
        for a in range(4)
    ]
    for a in range(4):
        own[a].start()
    parts = chips // GROUP
    part = place // GROUP

    for group in ((0, 4), (1,), (3,), (2,)):
        @pl.loop(1, chips)
        def _(j):
            for a in group:
                block_copy(a, j).start()
    for a in range(4):
        own[a].wait()

    def swap(n, core, m):
        ref = (kb, vb)[n].at[core, pl.ds(m * GROUP, GROUP)]
        return pltpu.make_async_remote_copy(
            src_ref=ref, dst_ref=ref, send_sem=swap_send.at[n, m], recv_sem=swap_recv.at[n, m],
            device_id=sibling, device_id_type=MESH,
        )

    def arrive(a):
        @pl.loop(1, chips)
        def _(j):
            arrival(a, (place + j) % chips).wait_recv()

    def arrive_and_swap(a, n):
        @pl.loop(0, parts)
        def _(v):
            m = (part + parts // 2 + parts - v) % parts
            for d in range(GROUP):
                @pl.when(m * GROUP + d != place)
                def _():
                    arrival(a, m * GROUP + d).wait_recv()

            swap(n, c, m).start()

    def swapped(n):
        @pl.loop(0, parts)
        def _(m):
            swap(n, 1 - c, m).wait_recv()

    arrive_and_swap(0, 0)
    arrive(4)

    rows = lax.broadcasted_iota(jnp.int32, (8 * chips, chips * BLOCK_TOKENS), 0)
    cols = lax.broadcasted_iota(jnp.int32, (8 * chips, chips * BLOCK_TOKENS), 1)
    spread = jnp.where(rows == 8 * (cols // BLOCK_TOKENS), 1.0, 0.0)
    counts = contract(cb[...].reshape(8 * chips, 128), spread, 0, 0)[: 2 * chips]
    logs = jnp.where(counts > 0.5, jnp.log(jnp.maximum(counts, 1.0)), NEG_FILL)
    width = GROUP * BLOCK_TOKENS
    for u in range(chips // GROUP):
        bias[u] = logs[:, u * width : (u + 1) * width]

    dka[...] = jnp.zeros_like(dka)
    dva[...] = jnp.zeros_like(dva)
    arrive(1)
    swapped(0)

    total = 2 * chips * BLOCK_TOKENS
    scale = 1.0 / math.sqrt(HEAD_SIZE)

    @pl.loop(0, parts)
    def _(u):
        keys = kb[...].reshape(total, HEAD_SIZE)
        query = qb[pl.ds(u * GROUP, GROUP)].reshape(width, HEAD_SIZE)
        score = contract(keys, query, 1, 1).reshape(2 * chips, BLOCK_TOKENS, width)
        score = (score * scale + bias[u][:, None, :]).reshape(total, width)
        power = jnp.exp(score - jnp.max(score, axis=0, keepdims=True))
        probs[u] = power * (1.0 / jnp.sum(power, axis=0, keepdims=True))

    arrive(3)

    @pl.loop(0, parts)
    def _(u):
        cotan = gb[pl.ds(u * GROUP, GROUP)].reshape(width, HEAD_SIZE)
        low = probs[u].astype(jnp.bfloat16)
        dva[...] += contract(low, cotan, 1, 0).reshape(dva.shape)

    def grad_copy(n):
        return pltpu.make_async_remote_copy(
            src_ref=(dka, dva)[n].at[1 - c], dst_ref=(dkr, dvr)[n],
            send_sem=grad_send.at[n], recv_sem=grad_recv.at[n],
            device_id=sibling, device_id_type=MESH,
        )

    grad_copy(1).start()

    results = (out_ref, dq_ref, dk_ref, dv_ref)
    out_core, out_slot = s // per_out, s % per_out

    def out_copy(a, t):
        lanes = pl.ds(pl.multiple_of(out_slot * HEAD_SIZE, HEAD_SIZE), HEAD_SIZE)
        return pltpu.make_async_remote_copy(
            src_ref=stage.at[a, t], dst_ref=results[a].at[:, c, :, lanes],
            send_sem=out_send.at[a, t], recv_sem=out_recv.at[a, out_slot, c],
            device_id=(t, 2 * x + out_core), device_id_type=MESH,
        )

    def out_own(a):
        lanes = pl.ds(pl.multiple_of(out_slot * HEAD_SIZE, HEAD_SIZE), HEAD_SIZE)
        return pltpu.make_async_copy(
            stage.at[a, s], results[a].at[:, c, :, lanes], own_sem.at[a]
        )

    def stays(t):
        return (out_core == c) & (t == s)

    def send_out(a, t):
        @pl.when(stays(t))
        def _():
            out_own(a).start()

        @pl.when(jnp.logical_not(stays(t)))
        def _():
            out_copy(a, t).start()

    def send_grad(n):
        grad_copy(n).wait_recv()
        final = (dka, dva)[n][c] + (dkr, dvr)[n][...]
        stage[2 + n] = final.astype(jnp.bfloat16).reshape(stage.shape[1:])

        @pl.loop(0, seq)
        def _(j):
            send_out(2 + n, (s + 3 + 3 * j) % seq)

    arrive_and_swap(2, 1)
    send_grad(1)
    swapped(1)
    shards_each = GROUP // planes

    @pl.loop(0, parts)
    def _(v):
        u = (part + 1 + v) % parts
        keys = kb[...].reshape(total, HEAD_SIZE)
        values = vb[...].reshape(total, HEAD_SIZE)
        query = qb[pl.ds(u * GROUP, GROUP)].reshape(width, HEAD_SIZE)
        cotan = gb[pl.ds(u * GROUP, GROUP)].reshape(width, HEAD_SIZE)
        prob = probs[u]
        halves = (shards_each, planes, BLOCK_TOKENS, HEAD_SIZE)
        slot = pl.ds(u * shards_each, shards_each)
        attended = contract(prob.astype(jnp.bfloat16), values, 0, 0)
        stage[0, slot] = attended.astype(jnp.bfloat16).reshape(halves)
        for d in range(shards_each):
            send_out(0, u * shards_each + d)
        dprob = contract(values, cotan, 1, 1)
        delta = jnp.sum(prob * dprob, axis=0, keepdims=True)
        dscore = (prob * (dprob - delta) * scale).astype(jnp.bfloat16)
        dquery = contract(dscore, keys, 0, 0)
        stage[1, slot] = dquery.astype(jnp.bfloat16).reshape(halves)
        for d in range(shards_each):
            send_out(1, u * shards_each + d)
        dka[...] += contract(dscore, query, 1, 0).reshape(dka.shape)

    grad_copy(0).start()
    send_grad(0)

    for a in range(5):
        @pl.loop(1, chips)
        def _(j):
            block_copy(a, j).wait_send()
    for n in range(2):
        @pl.loop(0, parts)
        def _(m):
            swap(n, c, m).wait_send()

        grad_copy(n).wait_send()
    for a in range(4):
        @pl.loop(0, seq)
        def _(t):
            @pl.when(stays(t))
            def _():
                out_own(a).wait()

            @pl.when(jnp.logical_not(stays(t)))
            def _():
                out_copy(a, t).wait_send()

        for d in range(per_out):
            for core in range(2):
                @pl.when(jnp.logical_not((s == c * per_out + d) & (core == c)))
                def _():
                    lanes = pl.ds(d * HEAD_SIZE, HEAD_SIZE)
                    ref = results[a].at[:, core, :, lanes]
                    pltpu.make_async_remote_copy(
                        src_ref=stage.at[a, 0], dst_ref=ref, send_sem=out_send.at[a, 0],
                        recv_sem=out_recv.at[a, d, core],
                        device_id=sibling, device_id_type=MESH,
                    ).wait_recv()


def by_head(seq, heads, queries, keys, values, cotangent, random_blocks, global_blocks):
    rows, feat = queries.shape
    planes = heads // 2
    chips = seq * planes
    per_out = feat // HEAD_SIZE // heads
    half = chips * rows
    low, wide = jnp.bfloat16, jnp.float32
    dma = pltpu.SemaphoreType.DMA
    shape = jax.ShapeDtypeStruct((planes, 2, rows, per_out * HEAD_SIZE), low)
    blocks = (chips, rows, HEAD_SIZE)
    flops = 6 * 2 * half * 2 * half * HEAD_SIZE
    results = pl.pallas_call(
        functools.partial(head_kernel, seq, heads, per_out),
        out_shape=[shape] * 4,
        in_specs=[pl.BlockSpec(memory_space=pl.ANY)] * 4
        + [pl.BlockSpec(memory_space=pltpu.SMEM)] * 2,
        out_specs=[pl.BlockSpec(memory_space=pl.ANY)] * 4,
        scratch_shapes=[
            pltpu.VMEM((2,) + blocks, low),
            pltpu.VMEM(blocks, low),
            pltpu.VMEM((2,) + blocks, low),
            pltpu.VMEM(blocks, low),
            pltpu.VMEM((chips, 8, 128), wide),
            pltpu.VMEM((chips // GROUP, 2 * chips, GROUP * rows), wide),
            pltpu.VMEM((chips // GROUP, 2 * half, GROUP * rows), wide),
            pltpu.VMEM((2, half, HEAD_SIZE), wide),
            pltpu.VMEM((2, half, HEAD_SIZE), wide),
            pltpu.VMEM((half, HEAD_SIZE), wide),
            pltpu.VMEM((half, HEAD_SIZE), wide),
            pltpu.VMEM((4, seq, planes, rows, HEAD_SIZE), low),
            pltpu.VMEM((rows, feat), low),
            pltpu.VMEM((rows, feat), low),
            pltpu.VMEM((rows, feat), low),
            pltpu.VMEM((rows, feat), low),
            dma((5, chips)),
            dma((5, chips)),
            dma((4,)),
            dma((2, chips // GROUP)),
            dma((2, chips // GROUP)),
            dma((2,)),
            dma((2,)),
            dma((4, seq)),
            dma((4, per_out, 2)),
        ],
        compiler_params=pltpu.CompilerParams(
            collective_id=0, has_side_effects=True, vmem_limit_bytes=63 * 2**20
        ),
        cost_estimate=pl.CostEstimate(
            flops=flops, bytes_accessed=16 * rows * feat, transcendentals=2 * half * half
        ),
    )(keys, queries, values, cotangent, random_blocks, global_blocks)
    return tuple(r.reshape(2 * planes * rows, per_out * HEAD_SIZE) for r in results)


def shards_or_heads(queries, keys, values, cotangent, random_blocks, global_blocks):
    seq, heads = lax.axis_size("seq"), lax.axis_size("head")
    rows, feat = queries.shape
    count = feat // HEAD_SIZE
    one_each = heads == 4 and 2 * count == seq * heads and rows == BLOCK_TOKENS
    args = (queries, keys, values, cotangent, random_blocks, global_blocks)
    if one_each and seq == 2 * (count // heads):
        return by_head(seq, heads, *args)
    return shards(*args)


def solution(mesh):
    in_specs = (
        P(("seq", "head"), None),
        P(("seq", "head"), None),
        P(("seq", "head"), None),
        P(("seq", "head"), None),
        P("seq", None),
        P(),
    )
    out_specs = (P("seq", "head"), P("seq", "head"), P("seq", "head"), P("seq", "head"))
    return jax.shard_map(
        shards_or_heads, mesh=mesh, in_specs=in_specs, out_specs=out_specs, check_vma=False
    )
```

```python
import functools
import math

import jax
import jax.numpy as jnp
from jax import lax
from jax.experimental import pallas as pl
from jax.experimental.pallas import tpu as pltpu
from jax.sharding import PartitionSpec as P

HEAD_SIZE = 128
BLOCK_TOKENS = 64
GLOB = 2
RAND = 3


NEG_FILL = -1e30


def padded(shard, sides, width):
    for axis, dim in sides:
        size, length = (lax.axis_size(axis), shard.shape[dim])
        up = [(i, (i + 1) % size) for i in range(size - 1)]
        down = [(j, i) for i, j in up]
        last = lax.slice_in_dim(shard, length - width, length, axis=dim)
        leading = lax.slice_in_dim(shard, 0, width, axis=dim)
        before = lax.ppermute(last, axis, up)
        after = lax.ppermute(leading, axis, down)
        shard = jnp.concatenate([before, shard, after], axis=dim)
    return shard


def broadcast(block, axis, source):
    block = jnp.where(lax.axis_index(axis) == source, block, jnp.zeros_like(block))
    return lax.psum(block, axis)


def entry_ranks(owner_ids):
    count = owner_ids.shape[-1]
    earlier = jnp.arange(count)[None, :] < jnp.arange(count)[:, None]
    same_owner = owner_ids[..., :, None] == owner_ids[..., None, :]
    return jnp.sum((same_owner & earlier).astype(jnp.int32), axis=-1)


def spread_band(band_part):
    return (
        jnp.pad(band_part[:, 0], ((0, 2), (0, 0), (0, 0)))
        + jnp.pad(band_part[:, 1], ((1, 1), (0, 0), (0, 0)))
        + jnp.pad(band_part[:, 2], ((2, 0), (0, 0), (0, 0)))
    )


def shards(queries, keys, values, cotangent, random_blocks, global_blocks):
    query_rows, gathered_keys, gathered_values, cotan_rows = (
        lax.all_to_all(queries, "head", split_axis=1, concat_axis=0, tiled=True),
        lax.all_to_all(keys, "head", split_axis=1, concat_axis=0, tiled=True),
        lax.all_to_all(values, "head", split_axis=1, concat_axis=0, tiled=True),
        lax.all_to_all(cotangent, "head", split_axis=1, concat_axis=0, tiled=True),
    )
    row_count, width = query_rows.shape
    head_count = width // HEAD_SIZE
    block_count = row_count // BLOCK_TOKENS
    shard_count = lax.axis_size("seq")
    my_index = lax.axis_index("seq")
    entry_count = block_count * RAND
    slot_cap = (3 * entry_count + 2 * shard_count - 1) // (2 * shard_count)
    slot_count = shard_count * slot_cap
    key_block_sets = 3 + GLOB + RAND
    logit_scale = 1.0 / math.sqrt(HEAD_SIZE)
    key_value = jnp.stack([gathered_keys, gathered_values])
    widened = padded(key_value, (("seq", 1),), BLOCK_TOKENS)
    widened = widened.reshape(2, block_count + 2, BLOCK_TOKENS, width)
    band_rows = jnp.stack([widened[:, :-2], widened[:, 1:-1], widened[:, 2:]], axis=2)
    own_blocks = key_value.reshape(2, block_count, BLOCK_TOKENS, width)
    owner_global = global_blocks // block_count
    local_global = global_blocks % block_count
    fetched = []
    for number in range(GLOB):
        mine = jnp.take(own_blocks, local_global[number], axis=1)
        fetched.append(broadcast(mine, "seq", owner_global[number]))
    global_rows = jnp.stack(fetched, axis=1)
    entry_ids = random_blocks.reshape(entry_count)
    owner_ids = entry_ids // block_count
    slot_ids = owner_ids * slot_cap + entry_ranks(owner_ids)
    slot_hits = slot_ids[None, :] == jnp.arange(slot_count)[:, None]
    filled = jnp.any(slot_hits, axis=1)
    source = jnp.sum(jnp.where(slot_hits, jnp.arange(entry_count)[None, :], 0), axis=1)
    wanted = jnp.sum(jnp.where(slot_hits, (entry_ids % block_count)[None, :], 0), axis=1)
    asked_ids = lax.all_to_all(wanted, "seq", split_axis=0, concat_axis=0, tiled=True)
    outgoing = jnp.take(own_blocks, asked_ids, axis=1)
    incoming = lax.all_to_all(outgoing, "seq", split_axis=1, concat_axis=1, tiled=True)
    random_rows = jnp.take(incoming, slot_ids, axis=1).reshape(
        2, block_count, RAND, BLOCK_TOKENS, width
    )

    def assemble_keys(which):
        spread_global = jnp.broadcast_to(
            global_rows[which][None], (block_count, GLOB, BLOCK_TOKENS, width)
        )
        joined = jnp.concatenate([band_rows[which], spread_global, random_rows[which]], axis=1)
        return joined.reshape(block_count, key_block_sets * BLOCK_TOKENS, head_count, HEAD_SIZE)

    key_all = assemble_keys(0)
    value_all = assemble_keys(1)
    block_number = my_index * block_count + jnp.arange(block_count)
    total_blocks = shard_count * block_count
    always = jnp.ones((block_count,), dtype=bool)
    group_ok = jnp.stack(
        [block_number >= 1, always, block_number <= total_blocks - 2] + [always] * (GLOB + RAND),
        axis=1,
    )
    valid_keys = jnp.repeat(group_ok, BLOCK_TOKENS, axis=1)[:, None, None, :]
    query_blocks = query_rows.reshape(block_count, BLOCK_TOKENS, head_count, HEAD_SIZE)
    cotan_blocks = cotan_rows.reshape(block_count, BLOCK_TOKENS, head_count, HEAD_SIZE)
    score_matrix = (
        jnp.einsum("bqhd,bkhd->bhqk", query_blocks, key_all, preferred_element_type=jnp.float32)
        * logit_scale
    )
    score_matrix = jnp.where(valid_keys, score_matrix, NEG_FILL)
    row_peak = jnp.max(score_matrix, axis=-1, keepdims=True)
    exponent = jnp.exp(score_matrix - row_peak)
    weights = exponent / jnp.sum(exponent, axis=-1, keepdims=True)
    weights_low = weights.astype(jnp.bfloat16)
    attended_output = jnp.einsum(
        "bhqk,bkhd->bqhd", weights_low, value_all, preferred_element_type=jnp.float32
    ).astype(jnp.bfloat16)
    weight_gradient = jnp.einsum(
        "bqhd,bkhd->bhqk", cotan_blocks, value_all, preferred_element_type=jnp.float32
    )
    row_delta = jnp.sum(weights * weight_gradient, axis=-1, keepdims=True)
    score_grad = (weights * (weight_gradient - row_delta) * logit_scale).astype(jnp.bfloat16)
    query_gradient = jnp.einsum(
        "bhqk,bkhd->bqhd", score_grad, key_all, preferred_element_type=jnp.float32
    ).astype(jnp.bfloat16)

    def part_grads(first, count):
        low_key = first * BLOCK_TOKENS
        high_key = (first + count) * BLOCK_TOKENS
        key_part = jnp.einsum(
            "bhqk,bqhd->bkhd",
            score_grad[..., low_key:high_key],
            query_blocks,
            preferred_element_type=jnp.float32,
        )
        value_part = jnp.einsum(
            "bhqk,bqhd->bkhd",
            weights_low[..., low_key:high_key],
            cotan_blocks,
            preferred_element_type=jnp.float32,
        )
        return (
            key_part.reshape(block_count, count, BLOCK_TOKENS, width),
            value_part.reshape(block_count, count, BLOCK_TOKENS, width),
        )

    band_key, band_value = part_grads(0, 3)
    extended_key = spread_band(band_key)
    extended_value = spread_band(band_value)
    rim_pair = jnp.stack(
        [
            jnp.stack([extended_key[0], extended_key[-1]]),
            jnp.stack([extended_value[0], extended_value[-1]]),
        ]
    )
    rimmed = padded(rim_pair.astype(jnp.bfloat16), (("seq", 1),), 1).astype(rim_pair.dtype)
    key_local = extended_key[1:-1].at[0].add(rimmed[0, 0]).at[-1].add(rimmed[0, 3])
    value_local = extended_value[1:-1].at[0].add(rimmed[1, 0]).at[-1].add(rimmed[1, 3])
    global_key, global_value = part_grads(3, GLOB)
    total_key, total_value = lax.psum(
        (jnp.sum(global_key, axis=0), jnp.sum(global_value, axis=0)), "seq"
    )
    for number in range(GLOB):
        owned = owner_global[number] == my_index
        key_local = key_local.at[local_global[number]].add(jnp.where(owned, total_key[number], 0.0))
        value_local = value_local.at[local_global[number]].add(
            jnp.where(owned, total_value[number], 0.0)
        )
    random_key, random_value = part_grads(3 + GLOB, RAND)
    keep = filled[:, None, None]
    send_key = jnp.where(
        keep, jnp.take(random_key.reshape(entry_count, BLOCK_TOKENS, width), source, axis=0), 0.0
    ).astype(jnp.bfloat16)
    send_value = jnp.where(
        keep, jnp.take(random_value.reshape(entry_count, BLOCK_TOKENS, width), source, axis=0), 0.0
    ).astype(jnp.bfloat16)
    arrived_key, arrived_value = (
        lax.all_to_all(send_key, "seq", split_axis=0, concat_axis=0, tiled=True),
        lax.all_to_all(send_value, "seq", split_axis=0, concat_axis=0, tiled=True),
    )
    owner_hits = (asked_ids[None, :] == jnp.arange(block_count)[:, None]).astype(jnp.float32)
    key_local = key_local + jnp.einsum(
        "js,srf->jrf", owner_hits, arrived_key.astype(jnp.float32), precision=lax.Precision.HIGHEST
    )
    value_local = value_local + jnp.einsum(
        "js,srf->jrf",
        owner_hits,
        arrived_value.astype(jnp.float32),
        precision=lax.Precision.HIGHEST,
    )
    return (
        attended_output.reshape(row_count, width),
        query_gradient.reshape(row_count, width),
        key_local.reshape(row_count, width).astype(jnp.bfloat16),
        value_local.reshape(row_count, width).astype(jnp.bfloat16),
    )


MESH = pl.DeviceIdType.MESH
GROUP = 4


def contract(a, b, dim_a, dim_b):
    return lax.dot_general(
        a, b, (((dim_a,), (dim_b,)), ((), ())), preferred_element_type=jnp.float32
    )


def head_kernel(
    seq, heads, per_out,
    k_ref, q_ref, v_ref, g_ref, random_ref, global_ref,
    out_ref,
    kb, qb, vb, gb, cb, bias, probs, dka, dva, dkr, dvr, stage,
    kin, qin, vin, gin, send_sem, recv_sem, own_sem, swap_send, swap_recv, grad_send, grad_recv,
    out_send, out_recv,
):
    s = lax.axis_index("seq")
    h = lax.axis_index("head")
    x, c = h // 2, h % 2
    planes = heads // 2
    chips = seq * planes
    devices = seq * heads
    me = s * heads + h
    place = s * planes + x
    sources = (kin, qin, vin, gin)
    loads = [
        pltpu.make_async_copy(ref, sources[a], own_sem.at[a])
        for a, ref in enumerate((k_ref, q_ref, v_ref, g_ref))
    ]
    for load in loads:
        load.start()
    landing = (kb.at[c], qb, vb.at[c], gb)
    sibling = (s, 2 * x + 1 - c)

    barrier = pltpu.get_barrier_semaphore()

    @pl.loop(1, devices)
    def _(j):
        to = (me + j) % devices
        pl.semaphore_signal(
            barrier, inc=1, device_id=(to // heads, to % heads), device_id_type=MESH
        )

    lane = lax.broadcasted_iota(jnp.int32, (8, 128), 1)
    block = jnp.where(lane < chips, 2 * lane, 2 * (lane - chips) + 1)
    block = jnp.where(lane < 2 * chips, block, -9)
    mine = s * heads + h
    entries = [mine - 1, mine, mine + 1]
    entries += [global_ref[e] for e in range(GLOB)]
    entries += [random_ref[h, e] for e in range(RAND)]
    count = jnp.zeros((8, 128), jnp.float32)
    for entry in entries:
        count = count + jnp.where(block == entry, 1.0, 0.0)
    cb[place] = count

    for load in loads:
        load.wait()
    pl.semaphore_wait(barrier, devices - 1)

    def columns(to_s, to_x):
        return pl.ds(pl.multiple_of((seq * to_x + to_s) * HEAD_SIZE, HEAD_SIZE), HEAD_SIZE)

    def block_copy(a, j):
        to = (place + j) % chips
        to_s, to_x = to // planes, to % planes
        if a < 4:
            src, dst = sources[a].at[:, columns(to_s, to_x)], landing[a].at[place]
        else:
            src, dst = cb.at[place], cb.at[place]
        return pltpu.make_async_remote_copy(
            src_ref=src, dst_ref=dst, send_sem=send_sem.at[a, j], recv_sem=recv_sem.at[a, place],
            device_id=(to_s, 2 * to_x + c), device_id_type=MESH,
        )

    def arrival(a, p):
        ref = landing[a].at[p] if a < 4 else cb.at[p]
        return pltpu.make_async_remote_copy(
            src_ref=ref, dst_ref=ref, send_sem=send_sem.at[a, 0], recv_sem=recv_sem.at[a, p],
            device_id=sibling, device_id_type=MESH,
        )

    own = [
        pltpu.make_async_copy(
            sources[a].at[:, columns(s, x)], landing[a].at[place], own_sem.at[a]
        )
        for a in range(4)
    ]
    for a in range(4):
        own[a].start()
    parts = chips // GROUP
    part = place // GROUP

    for group in ((0, 4), (1,), (3,), (2,)):
        @pl.loop(1, chips)
        def _(j):
            for a in group:
                block_copy(a, j).start()
    for a in range(4):
        own[a].wait()

    def swap(n, core, m):
        ref = (kb, vb)[n].at[core, pl.ds(m * GROUP, GROUP)]
        return pltpu.make_async_remote_copy(
            src_ref=ref, dst_ref=ref, send_sem=swap_send.at[n, m], recv_sem=swap_recv.at[n, m],
            device_id=sibling, device_id_type=MESH,
        )

    def arrive(a):
        @pl.loop(1, chips)
        def _(j):
            arrival(a, (place + j) % chips).wait_recv()

    def arrive_and_swap(a, n):
        @pl.loop(0, parts)
        def _(v):
            m = (part + parts // 2 + parts - v) % parts
            for d in range(GROUP):
                @pl.when(m * GROUP + d != place)
                def _():
                    arrival(a, m * GROUP + d).wait_recv()

            swap(n, c, m).start()

    def swapped(n):
        @pl.loop(0, parts)
        def _(m):
            swap(n, 1 - c, m).wait_recv()

    arrive_and_swap(0, 0)
    arrive(4)

    rows = lax.broadcasted_iota(jnp.int32, (8 * chips, chips * BLOCK_TOKENS), 0)
    cols = lax.broadcasted_iota(jnp.int32, (8 * chips, chips * BLOCK_TOKENS), 1)
    spread = jnp.where(rows == 8 * (cols // BLOCK_TOKENS), 1.0, 0.0)
    counts = contract(cb[...].reshape(8 * chips, 128), spread, 0, 0)[: 2 * chips]
    logs = jnp.where(counts > 0.5, jnp.log(jnp.maximum(counts, 1.0)), NEG_FILL)
    width = GROUP * BLOCK_TOKENS
    for u in range(chips // GROUP):
        bias[u] = logs[:, u * width : (u + 1) * width]

    dka[...] = jnp.zeros_like(dka)
    dva[...] = jnp.zeros_like(dva)
    arrive(1)
    swapped(0)

    total = 2 * chips * BLOCK_TOKENS
    scale = 1.0 / math.sqrt(HEAD_SIZE)

    @pl.loop(0, parts)
    def _(u):
        keys = kb[...].reshape(total, HEAD_SIZE)
        query = qb[pl.ds(u * GROUP, GROUP)].reshape(width, HEAD_SIZE)
        score = contract(keys, query, 1, 1).reshape(2 * chips, BLOCK_TOKENS, width)
        score = (score * scale + bias[u][:, None, :]).reshape(total, width)
        power = jnp.exp(score - jnp.max(score, axis=0, keepdims=True))
        probs[u] = power * (1.0 / jnp.sum(power, axis=0, keepdims=True))

    arrive(3)

    @pl.loop(0, parts)
    def _(u):
        cotan = gb[pl.ds(u * GROUP, GROUP)].reshape(width, HEAD_SIZE)
        low = probs[u].astype(jnp.bfloat16)
        dva[...] += contract(low, cotan, 1, 0).reshape(dva.shape)

    def grad_copy(n):
        return pltpu.make_async_remote_copy(
            src_ref=(dka, dva)[n].at[1 - c], dst_ref=(dkr, dvr)[n],
            send_sem=grad_send.at[n], recv_sem=grad_recv.at[n],
            device_id=sibling, device_id_type=MESH,
        )

    grad_copy(1).start()

    results = tuple(out_ref.at[a] for a in range(4))
    out_core, out_slot = s // per_out, s % per_out

    def out_copy(a, t):
        lanes = pl.ds(pl.multiple_of(out_slot * HEAD_SIZE, HEAD_SIZE), HEAD_SIZE)
        return pltpu.make_async_remote_copy(
            src_ref=stage.at[a, t], dst_ref=results[a].at[:, c, :, lanes],
            send_sem=out_send.at[a, t], recv_sem=out_recv.at[a, out_slot, c],
            device_id=(t, 2 * x + out_core), device_id_type=MESH,
        )

    def out_own(a):
        lanes = pl.ds(pl.multiple_of(out_slot * HEAD_SIZE, HEAD_SIZE), HEAD_SIZE)
        return pltpu.make_async_copy(
            stage.at[a, s], results[a].at[:, c, :, lanes], own_sem.at[a]
        )

    def stays(t):
        return (out_core == c) & (t == s)

    def send_out(a, t):
        @pl.when(stays(t))
        def _():
            out_own(a).start()

        @pl.when(jnp.logical_not(stays(t)))
        def _():
            out_copy(a, t).start()

    def send_grad(n):
        grad_copy(n).wait_recv()
        final = (dka, dva)[n][c] + (dkr, dvr)[n][...]
        stage[2 + n] = final.astype(jnp.bfloat16).reshape(stage.shape[1:])

        @pl.loop(0, seq)
        def _(j):
            send_out(2 + n, (s + 3 + 3 * j) % seq)

    arrive_and_swap(2, 1)
    send_grad(1)
    swapped(1)
    shards_each = GROUP // planes

    @pl.loop(0, parts)
    def _(v):
        u = (part + 1 + v) % parts
        keys = kb[...].reshape(total, HEAD_SIZE)
        values = vb[...].reshape(total, HEAD_SIZE)
        query = qb[pl.ds(u * GROUP, GROUP)].reshape(width, HEAD_SIZE)
        cotan = gb[pl.ds(u * GROUP, GROUP)].reshape(width, HEAD_SIZE)
        prob = probs[u]
        halves = (shards_each, planes, BLOCK_TOKENS, HEAD_SIZE)
        slot = pl.ds(u * shards_each, shards_each)
        attended = contract(prob.astype(jnp.bfloat16), values, 0, 0)
        stage[0, slot] = attended.astype(jnp.bfloat16).reshape(halves)
        for d in range(shards_each):
            send_out(0, u * shards_each + d)
        dprob = contract(values, cotan, 1, 1)
        delta = jnp.sum(prob * dprob, axis=0, keepdims=True)
        dscore = (prob * (dprob - delta) * scale).astype(jnp.bfloat16)
        dquery = contract(dscore, keys, 0, 0)
        stage[1, slot] = dquery.astype(jnp.bfloat16).reshape(halves)
        for d in range(shards_each):
            send_out(1, u * shards_each + d)
        dka[...] += contract(dscore, query, 1, 0).reshape(dka.shape)

    grad_copy(0).start()
    send_grad(0)

    for a in range(5):
        @pl.loop(1, chips)
        def _(j):
            block_copy(a, j).wait_send()
    for n in range(2):
        @pl.loop(0, parts)
        def _(m):
            swap(n, c, m).wait_send()

        grad_copy(n).wait_send()
    for a in range(4):
        @pl.loop(0, seq)
        def _(t):
            @pl.when(stays(t))
            def _():
                out_own(a).wait()

            @pl.when(jnp.logical_not(stays(t)))
            def _():
                out_copy(a, t).wait_send()

        for d in range(per_out):
            for core in range(2):
                @pl.when(jnp.logical_not((s == c * per_out + d) & (core == c)))
                def _():
                    lanes = pl.ds(d * HEAD_SIZE, HEAD_SIZE)
                    ref = results[a].at[:, core, :, lanes]
                    pltpu.make_async_remote_copy(
                        src_ref=stage.at[a, 0], dst_ref=ref, send_sem=out_send.at[a, 0],
                        recv_sem=out_recv.at[a, d, core],
                        device_id=sibling, device_id_type=MESH,
                    ).wait_recv()


def by_head(seq, heads, queries, keys, values, cotangent, random_blocks, global_blocks):
    rows, feat = queries.shape
    planes = heads // 2
    chips = seq * planes
    per_out = feat // HEAD_SIZE // heads
    half = chips * rows
    low, wide = jnp.bfloat16, jnp.float32
    dma = pltpu.SemaphoreType.DMA
    shape = jax.ShapeDtypeStruct((4, planes, 2, rows, per_out * HEAD_SIZE), low)
    blocks = (chips, rows, HEAD_SIZE)
    flops = 6 * 2 * half * 2 * half * HEAD_SIZE
    results = pl.pallas_call(
        functools.partial(head_kernel, seq, heads, per_out),
        out_shape=shape,
        in_specs=[pl.BlockSpec(memory_space=pl.ANY)] * 4
        + [pl.BlockSpec(memory_space=pltpu.SMEM)] * 2,
        out_specs=pl.BlockSpec(memory_space=pl.ANY),
        scratch_shapes=[
            pltpu.VMEM((2,) + blocks, low),
            pltpu.VMEM(blocks, low),
            pltpu.VMEM((2,) + blocks, low),
            pltpu.VMEM(blocks, low),
            pltpu.VMEM((chips, 8, 128), wide),
            pltpu.VMEM((chips // GROUP, 2 * chips, GROUP * rows), wide),
            pltpu.VMEM((chips // GROUP, 2 * half, GROUP * rows), wide),
            pltpu.VMEM((2, half, HEAD_SIZE), wide),
            pltpu.VMEM((2, half, HEAD_SIZE), wide),
            pltpu.VMEM((half, HEAD_SIZE), wide),
            pltpu.VMEM((half, HEAD_SIZE), wide),
            pltpu.VMEM((4, seq, planes, rows, HEAD_SIZE), low),
            pltpu.VMEM((rows, feat), low),
            pltpu.VMEM((rows, feat), low),
            pltpu.VMEM((rows, feat), low),
            pltpu.VMEM((rows, feat), low),
            dma((5, chips)),
            dma((5, chips)),
            dma((4,)),
            dma((2, chips // GROUP)),
            dma((2, chips // GROUP)),
            dma((2,)),
            dma((2,)),
            dma((4, seq)),
            dma((4, per_out, 2)),
        ],
        compiler_params=pltpu.CompilerParams(
            collective_id=0, has_side_effects=True, vmem_limit_bytes=63 * 2**20
        ),
        cost_estimate=pl.CostEstimate(
            flops=flops, bytes_accessed=16 * rows * feat, transcendentals=2 * half * half
        ),
    )(keys, queries, values, cotangent, random_blocks, global_blocks)
    return tuple(r.reshape(2 * planes * rows, per_out * HEAD_SIZE) for r in results)


def shards_or_heads(queries, keys, values, cotangent, random_blocks, global_blocks):
    seq, heads = lax.axis_size("seq"), lax.axis_size("head")
    rows, feat = queries.shape
    count = feat // HEAD_SIZE
    one_each = heads == 4 and 2 * count == seq * heads and rows == BLOCK_TOKENS
    args = (queries, keys, values, cotangent, random_blocks, global_blocks)
    if one_each and seq == 2 * (count // heads):
        return by_head(seq, heads, *args)
    return shards(*args)


def solution(mesh):
    in_specs = (
        P(("seq", "head"), None),
        P(("seq", "head"), None),
        P(("seq", "head"), None),
        P(("seq", "head"), None),
        P("seq", None),
        P(),
    )
    out_specs = (P("seq", "head"), P("seq", "head"), P("seq", "head"), P("seq", "head"))
    return jax.shard_map(
        shards_or_heads, mesh=mesh, in_specs=in_specs, out_specs=out_specs, check_vma=False
    )
```
